128 devices in a mesh: row: 8 (over z, x_lo), col: 16 (over y, x_hi, core).
Axes of the slice: x: 4 (x_hi: 2, x_lo: 2; x = x_hi * 2 + x_lo), y: 4, z: 4, core: 2. Of those that a mesh axis runs over, the one named last changes fastest.
Arguments:
- emb_first: float32 [40, 32768], P(None, ('row', 'col')), may hold values from -6 to 6
- emb_second: float32 [40, 32768], P(None, ('row', 'col')), may hold values from -6 to 6
- signal: float32 [32, 32768], P(None, ('row', 'col')), may hold values from -6 to 6
- theta_first: float32 [40, 40], replicated, may hold values from -1 to 1
- theta_second: float32 [40, 40], replicated, may hold values from -1 to 1
- neighbors: int32 [20, 32768], P(None, 'row'), may hold values from 0 to 32767, as said below
- w_forward: float32 [96, 32], replicated, may hold values from -0.625 to 0.625
- w_backward: float32 [96, 32], replicated, may hold values from -0.625 to 0.625
Outputs:
- mixed: float32 [32, 32768], P(None, ('row', 'col'))
The draws below stay inside these ranges and needn't reach their ends.
Inputs may be any that keep to these rules, and one draw needn't show every extreme that they name: For each node i the 20 entries neighbors[:, i] are distinct; entry k lies in the stretch of 32768 // 20 columns that begins k * (32768 // 20) columns after a start of its own for node i, counted cyclically over all 32768 columns.
All inputs are finite; a program needn't handle non-finite values.
Results may differ from the reference program's by a relative error of at most 0.00012.
Values sent between devices are 32-bit elements; how exact they have to be, the bound alone decides.
A program may use at most 128 MiB of HBM per device.

```python
import jax
import jax.numpy as jnp
from jax import lax

EMB = 40
FEAT = 32
FOUT = 32
TOPK = 20
DEPTH = 2
NODES = 32768


def draw_neighbors(key, part):
    stretch = NODES // TOPK
    key_start, key_offset = jax.random.split(key)
    first_col = jax.random.randint(key_start, (1, NODES), 0, NODES)
    offsets = jax.random.randint(key_offset, (TOPK, NODES), 0, stretch)
    stride = jnp.arange(TOPK, dtype=jnp.int32)[:, None] * stretch
    return ((first_col + stride + offsets) % NODES).astype(jnp.int32)


def levels(stream_key, extent, pieces, smallest, top_value):
    def one(position, blocks):
        draws = jax.random.uniform(jax.random.fold_in(jax.random.fold_in(stream_key, 6), position), (blocks,), jnp.float32, smallest / len(pieces), top_value / len(pieces))
        return jnp.repeat(jnp.exp(draws), extent[position] // blocks).reshape((-1,) + (1,) * (len(extent) - position - 1))

    level = one(*pieces[0])
    for cut in pieces[1:]:
        level = level * one(*cut)
    return level


def normal_values(own_key, dims, width, limit, shards=(), held_as=jnp.bfloat16):
    gain = levels(own_key, dims, shards, -0.22, 0.18) if shards else 1.0
    drawn = jax.random.normal(own_key, dims, jnp.float32) * width * gain
    return jnp.minimum(jnp.maximum(drawn, -limit), limit).astype(held_as)


def setup_inputs(seed: int = 0) -> dict:
    streams_of = jax.random.split(jax.random.key(seed), 9)
    return {
        "emb_first": normal_values(streams_of[0], (EMB, NODES), 1.0, 6.0, ((1, 128),), jnp.float32),
        "emb_second": normal_values(streams_of[1], (EMB, NODES), 1.0, 6.0, ((1, 128),), jnp.float32),
        "signal": normal_values(streams_of[2], (FEAT, NODES), 1.0, 6.0, ((1, 128),), jnp.float32),
        "theta_first": normal_values(streams_of[3], (EMB, EMB), EMB ** -0.5, 1.0, (), jnp.float32),
        "theta_second": normal_values(streams_of[4], (EMB, EMB), EMB ** -0.5, 1.0, (), jnp.float32),
        "neighbors": draw_neighbors(jax.random.fold_in(streams_of[8], 71), 0),
        "w_forward": normal_values(streams_of[6], ((DEPTH + 1) * FEAT, FOUT), ((DEPTH + 1) * FEAT) ** -0.5, 0.625, (), jnp.float32),
        "w_backward": normal_values(streams_of[7], ((DEPTH + 1) * FEAT, FOUT), ((DEPTH + 1) * FEAT) ** -0.5, 0.625, (), jnp.float32),
    }


def reference(emb_first, emb_second, signal, theta_first, theta_second, neighbors, w_forward, w_backward):
    highest = lax.Precision.HIGHEST
    m_first = jnp.tanh(3.0 * jnp.dot(theta_first.T, emb_first, precision=highest, preferred_element_type=jnp.float32))
    m_second = jnp.tanh(3.0 * jnp.dot(theta_second.T, emb_second, precision=highest, preferred_element_type=jnp.float32))
    score = jnp.sum(m_first[:, None, :] * jnp.take(m_second, neighbors, axis=1), axis=0)
    score = score - jnp.sum(m_second[:, None, :] * jnp.take(m_first, neighbors, axis=1), axis=0)
    edge_weight = jax.nn.relu(jnp.tanh(3.0 * score))
    flat_index = neighbors.reshape(-1).astype(jnp.int32)
    node_count = signal.shape[1]
    channels = signal.shape[0]
    degree_out = 1.0 + jnp.sum(edge_weight, axis=0)
    degree_in = 1.0 + jnp.zeros((node_count,), jnp.float32).at[flat_index].add(edge_weight.reshape(-1))
    fwd_list = [signal]
    current = signal
    for hop_index in range(DEPTH):
        gathered = jnp.sum(edge_weight[None, :, :] * jnp.take(current, neighbors, axis=1), axis=1)
        current = 0.05 * signal + 0.95 * (gathered + current) / degree_out[None, :]
        fwd_list.append(current)
    bwd_list = [signal]
    current = signal
    for hop_index in range(DEPTH):
        terms = (edge_weight[None, :, :] * current[:, None, :]).reshape(channels, -1)
        spread = jnp.zeros((channels, node_count), jnp.float32).at[:, flat_index].add(terms)
        current = 0.05 * signal + 0.95 * (spread + current) / degree_in[None, :]
        bwd_list.append(current)
    mixed = jnp.dot(w_forward.T, jnp.concatenate(fwd_list, axis=0), precision=highest, preferred_element_type=jnp.float32)
    mixed = mixed + jnp.dot(w_backward.T, jnp.concatenate(bwd_list, axis=0), precision=highest, preferred_element_type=jnp.float32)
    return mixed
```

```python
import jax
import jax.numpy as jnp
from jax import lax
from jax.experimental import pallas as pl
from jax.experimental.pallas import tpu as pltpu
from jax.sharding import PartitionSpec as P

KEEP = 0.05
GO = 1.0 - KEEP
HIGHEST = lax.Precision.HIGHEST
MESH = pl.DeviceIdType.MESH
f32, bf16, i32 = jnp.float32, jnp.bfloat16, jnp.int32

ROWS = 8
COLS = 16
B = 256
SLOTS = 3
EMB = 40
FEAT = 32
ALL = 2 * EMB + FEAT
PART = FEAT + 8


def halves(x):
    hi = x.astype(bf16).astype(f32)
    return hi, x - hi


def transposed_dot(a, b):
    return lax.dot_general(
        a, b, (((0,), (0,)), ((), ())), precision=HIGHEST, preferred_element_type=f32
    )


def kernel(
    emb_first, emb_second, signal, theta_first, theta_second, neighbors, w_forward, w_backward,
    out,
    emb1, emb2, theta1, theta2, near, wf, wb,
    home, rows, cols, right, left, xs, st, hot, idx, weight, acc,
    f_part, f_got, b_part, b_got, f_home, b_home, colx, rowx, f_part2, f_got2, b_part2, b_got2,
    in_sem, c_send, c_recv, r_send, r_recv, f_send, f_recv, b_send, b_recv,
    c2_send, c2_recv, r2_send, r2_recv, f2_send, f2_recv, b2_send, b2_recv,
):
    r = lax.axis_index("row")
    c = lax.axis_index("col")
    half = c // ROWS
    q = c % ROWS
    base = c - q
    user = base + r
    block_start = (2 * q + half) * (ROWS * B)
    same = q == r
    others = jnp.where(same, 0, 1).astype(i32)

    barrier = pltpu.get_barrier_semaphore()

    def greet(i, carry):
        pl.semaphore_signal(barrier, inc=1, device_id=(r, (c + i) % COLS), device_id_type=MESH)
        return carry

    def greet_columns(i, carry):
        k = (r + i) % ROWS

        @pl.when(jnp.logical_not(jnp.logical_and(same, k == r)))
        def _():
            pl.semaphore_signal(barrier, inc=1, device_id=(k, user), device_id_type=MESH)
            pl.semaphore_signal(barrier, inc=1, device_id=(q, base + k), device_id_type=MESH)

        return carry

    lax.fori_loop(1, COLS, greet, 0)
    lax.fori_loop(0, ROWS, greet_columns, 0)

    fetches = [
        pltpu.make_async_copy(src, dst, in_sem.at[n])
        for n, (src, dst) in enumerate(
            [
                (emb_first, emb1), (emb_second, emb2), (theta_first, theta1),
                (theta_second, theta2), (signal, home.at[pl.ds(2 * EMB, FEAT)]),
                (neighbors, near), (w_forward, wf), (w_backward, wb),
            ]
        )
    ]
    for fetch in fetches:
        fetch.start()
    for fetch in fetches[:5]:
        fetch.wait()
    home[0:EMB, :] = jnp.tanh(3.0 * transposed_dot(theta1[...], emb1[...]))
    home[EMB : 2 * EMB, :] = jnp.tanh(3.0 * transposed_dot(theta2[...], emb2[...]))

    pl.semaphore_wait(barrier, COLS - 1 + 2 * (ROWS - 1) + 2 * others)

    def to_users(k, src, dst, send, recv):
        return pltpu.make_async_remote_copy(
            src_ref=src, dst_ref=dst.at[q], send_sem=send.at[k], recv_sem=recv.at[q],
            device_id=(k, user), device_id_type=MESH,
        )

    def to_row(k, src, dst, send, recv):
        return pltpu.make_async_remote_copy(
            src_ref=src, dst_ref=dst.at[c], send_sem=send.at[k], recv_sem=recv.at[c],
            device_id=(r, k), device_id_type=MESH,
        )

    def to_homes(k, src, dst, send, recv):
        return pltpu.make_async_remote_copy(
            src_ref=src, dst_ref=dst.at[r], send_sem=send.at[k], recv_sem=recv.at[r],
            device_id=(q, base + k), device_id_type=MESH,
        )

    def arrival(dst, slot, send, recv):
        return pltpu.make_async_remote_copy(
            src_ref=dst.at[slot], dst_ref=dst.at[slot], send_sem=send.at[slot],
            recv_sem=recv.at[slot], device_id=(r, (c + 1) % COLS), device_id_type=MESH,
        )

    def share_with_users(src, dst, send, recv):
        def step(i, carry):
            k = (r + i) % ROWS

            @pl.when(jnp.logical_not(jnp.logical_and(same, k == r)))
            def _():
                to_users(k, src, dst, send, recv).start()

            return carry

        lax.fori_loop(0, ROWS, step, 0)

        @pl.when(same)
        def _():
            dst[q] = src[...]

    def from_homes(dst, send, recv):
        def step(k, carry):
            @pl.when(jnp.logical_not(jnp.logical_and(same, k == q)))
            def _():
                arrival(dst, k, send, recv).wait_recv()

            return carry

        lax.fori_loop(0, ROWS, step, 0)

    def share_with_row(src, dst, send, recv):
        def step(i, carry):
            to_row((c + COLS - i) % COLS, src, dst, send, recv).start()
            return carry

        lax.fori_loop(1, COLS, step, 0)
        dst[c] = src[...]

    share_with_users(home, cols, c_send, c_recv)
    share_with_row(home, rows, r_send, r_recv)

    fetches[5].wait()

    def find(g, carry):
        span = pl.ds(pl.multiple_of(g * B, B), B)
        local = near[:, span] - block_start
        slot = [jnp.full((1, B), -1, i32) for _ in range(SLOTS)]
        for k in range(near.shape[0]):
            entry = local[k : k + 1]
            inside = jnp.logical_and(entry >= 0, entry < ROWS * B)
            slot = [
                jnp.where(inside, entry, slot[0]),
                jnp.where(inside, slot[0], slot[1]),
                jnp.where(inside, slot[1], slot[2]),
            ]
        place = lax.broadcasted_iota(i32, (B, B), 0)
        for j in range(SLOTS):
            hot[g, :, j * B : (j + 1) * B] = (place == (slot[j] & (B - 1))).astype(f32).astype(bf16)
        idx[g] = jnp.concatenate(slot + [jnp.full((8 - SLOTS, B), -1, i32)], axis=0)
        return carry

    lax.fori_loop(0, COLS, find, 0)

    def put_columns(values, v):
        hi, lo = halves(values)
        xs[v * 64 : v * 64 + 64, :] = jnp.concatenate([hi, lo], axis=0).astype(bf16)

    from_homes(cols, c_send, c_recv)
    for v in range(ROWS):
        turned = jnp.concatenate([cols[v, EMB : 2 * EMB, :], -cols[v, 0:EMB, :]], axis=0)
        hi, lo = halves(turned)
        right[v * B : (v + 1) * B, :] = jnp.concatenate([hi, hi, lo], axis=0).T.astype(bf16)
        put_columns(cols[v, 2 * EMB : ALL, :], v)

    def forward(g):
        picked = jnp.dot(xs[...], hot[g], preferred_element_type=f32)
        total = jnp.zeros((FEAT, B), f32)
        for j in range(SLOTS):
            window = idx[g, j : j + 1, :] >> 8
            part = jnp.zeros((2 * FEAT, B), f32)
            for v in range(ROWS):
                part = jnp.where(
                    window == v, picked[v * 64 : v * 64 + 64, j * B : (j + 1) * B], part
                )
            total = total + weight[g, j : j + 1, :] * (part[:FEAT] + part[FEAT:])
        return total

    def first_step(i, carry):
        g = (c + i) % COLS

        @pl.when(i > 0)
        def _():
            arrival(rows, g, r_send, r_recv).wait_recv()

        hi, lo = halves(rows[g, 0 : 2 * EMB, :])
        left[...] = jnp.concatenate([hi, lo, hi], axis=0).astype(bf16)
        eight = lax.broadcasted_iota(i32, (8, B), 0)
        gap = [idx[g, j : j + 1, :] - eight for j in range(SLOTS)]
        found = [jnp.zeros((8, B), f32) for _ in range(SLOTS)]
        for v in range(ROWS):
            score = jnp.dot(
                right[v * B : (v + 1) * B, :], left[...], preferred_element_type=f32
            )
            for t in range(B // 8):
                for j in range(SLOTS):
                    found[j] = jnp.where(
                        gap[j] == v * B + 8 * t, score[8 * t : 8 * t + 8], found[j]
                    )
        sums = jnp.zeros((1, B), f32)
        for j in range(SLOTS):
            value = jnp.tanh(3.0 * jnp.sum(found[j], axis=0, keepdims=True))
            value = jnp.where(idx[g, j : j + 1, :] >= 0, jnp.maximum(value, 0.0), 0.0)
            weight[g, j : j + 1, :] = value
            sums = sums + value
        f_part[g, 0:FEAT, :] = forward(g)
        f_part[g, FEAT:PART, :] = jnp.broadcast_to(sums, (8, B))

        @pl.when(i > 0)
        def _():
            to_row(g, f_part.at[g], f_got, f_send, f_recv).start()

        return carry

    lax.fori_loop(0, COLS, first_step, 0)

    def backward(rows_of, ready, part, with_degree):
        acc[...] = jnp.zeros_like(acc)

        def step(i, carry):
            g = (c + i) % COLS
            ready(i, g)
            x = rows_of(g)
            for j in range(SLOTS):
                window = idx[g, j : j + 1, :] >> 8
                value = weight[g, j : j + 1, :]
                hi, lo = halves(x * value)
                both = jnp.concatenate([hi, lo], axis=0)
                for v in range(ROWS):
                    st[v * 64 : v * 64 + 64, j * B : (j + 1) * B] = jnp.where(
                        window == v, both, 0.0
                    ).astype(bf16)
                if with_degree:
                    hi, lo = halves(value)
                    mine = lax.broadcasted_iota(i32, (8, B), 0) == window
                    st[512:528, j * B : (j + 1) * B] = jnp.concatenate(
                        [jnp.where(mine, hi, 0.0), jnp.where(mine, lo, 0.0)], axis=0
                    ).astype(bf16)
            depth = 528 if with_degree else 512
            acc[0:depth, :] += lax.dot_general(
                st[0:depth, :], hot[g], (((1,), (1,)), ((), ())), preferred_element_type=f32
            )
            return carry

        lax.fori_loop(0, COLS, step, 0)
        for v in range(ROWS):
            part[v, 0:FEAT, :] = acc[v * 64 : v * 64 + 32, :] + acc[v * 64 + 32 : v * 64 + 64, :]
            if with_degree:
                part[v, FEAT:PART, :] = jnp.broadcast_to(
                    acc[512 + v : 513 + v, :] + acc[520 + v : 521 + v, :], (8, B)
                )

    def give_back(part, got, send, recv):
        def step(k, carry):
            @pl.when(jnp.logical_not(jnp.logical_and(same, k == q)))
            def _():
                to_homes(k, part.at[k], got, send, recv).start()

            return carry

        lax.fori_loop(0, ROWS, step, 0)

        @pl.when(same)
        def _():
            got[r] = part[q]

    def add_forward(part, got, send, recv):
        def step(i, total):
            k = (c + COLS - i) % COLS
            arrival(got, k, send, recv).wait_recv()
            return total + got[k]

        return lax.fori_loop(1, COLS, step, part[c])

    def add_backward(got, send, recv):
        def step(k, total):
            @pl.when(jnp.logical_not(jnp.logical_and(same, k == r)))
            def _():
                arrival(got, k, send, recv).wait_recv()

            return total + got[k]

        return lax.fori_loop(0, ROWS, step, jnp.zeros(got.shape[1:], f32))

    backward(lambda g: rows[g, 2 * EMB : ALL, :], lambda i, g: None, b_part, True)
    give_back(b_part, b_got, b_send, b_recv)

    own = home[2 * EMB : ALL, :]
    summed = add_forward(f_part, f_got, f_send, f_recv)
    f_scale = GO / (1.0 + summed[FEAT : FEAT + 1])
    f_home[...] = KEEP * own + (summed[:FEAT] + own) * f_scale
    share_with_users(f_home, colx, c2_send, c2_recv)

    summed = add_backward(b_got, b_send, b_recv)
    b_scale = GO / (1.0 + summed[FEAT : FEAT + 1])
    b_home[...] = KEEP * own + (summed[:FEAT] + own) * b_scale
    share_with_row(b_home, rowx, r2_send, r2_recv)

    from_homes(colx, c2_send, c2_recv)
    for v in range(ROWS):
        put_columns(colx[v], v)

    def second_step(i, carry):
        g = (c + i) % COLS
        f_part2[g] = forward(g)

        @pl.when(i > 0)
        def _():
            to_row(g, f_part2.at[g], f_got2, f2_send, f2_recv).start()

        return carry

    lax.fori_loop(0, COLS, second_step, 0)

    def ready(i, g):
        @pl.when(i > 0)
        def _():
            arrival(rowx, g, r2_send, r2_recv).wait_recv()

    backward(lambda g: rowx[g], ready, b_part2, False)
    give_back(b_part2, b_got2, b2_send, b2_recv)

    fetches[6].wait()
    fetches[7].wait()
    first = f_home[...]
    summed = add_forward(f_part2, f_got2, f2_send, f2_recv)
    second = KEEP * own + (summed + first) * f_scale
    mixed = transposed_dot(wf[...], jnp.concatenate([own, first, second], axis=0))
    first = b_home[...]
    summed = add_backward(b_got2, b2_send, b2_recv)
    second = KEEP * own + (summed + first) * b_scale
    out[...] = mixed + transposed_dot(wb[...], jnp.concatenate([own, first, second], axis=0))

    def sent_to_users(k, carry):
        @pl.when(jnp.logical_not(jnp.logical_and(same, k == r)))
        def _():
            to_users(k, home, cols, c_send, c_recv).wait_send()
            to_users(k, f_home, colx, c2_send, c2_recv).wait_send()

        @pl.when(jnp.logical_not(jnp.logical_and(same, k == q)))
        def _():
            to_homes(k, b_part.at[k], b_got, b_send, b_recv).wait_send()
            to_homes(k, b_part2.at[k], b_got2, b2_send, b2_recv).wait_send()

        return carry

    def sent_to_row(i, carry):
        k = (c + i) % COLS
        to_row(k, home, rows, r_send, r_recv).wait_send()
        to_row(k, f_part.at[k], f_got, f_send, f_recv).wait_send()
        to_row(k, b_home, rowx, r2_send, r2_recv).wait_send()
        to_row(k, f_part2.at[k], f_got2, f2_send, f2_recv).wait_send()
        return carry

    lax.fori_loop(0, ROWS, sent_to_users, 0)
    lax.fori_loop(1, COLS, sent_to_row, 0)


def per_device(*args):
    vmem = pltpu.VMEM
    keep_count = args[5].shape[0]
    dma = pltpu.SemaphoreType.DMA
    scratch = [
        vmem((EMB, B), f32), vmem((EMB, B), f32), vmem((EMB, EMB), f32), vmem((EMB, EMB), f32),
        vmem((keep_count, COLS * B), i32), vmem((3 * FEAT, FEAT), f32), vmem((3 * FEAT, FEAT), f32),
        vmem((ALL, B), f32),
        vmem((COLS, ALL, B), f32),
        vmem((ROWS, ALL, B), f32),
        vmem((ROWS * B, 6 * EMB), bf16),
        vmem((6 * EMB, B), bf16),
        vmem((512, B), bf16),
        vmem((528, SLOTS * B), bf16),
        vmem((COLS, B, SLOTS * B), bf16),
        vmem((COLS, 8, B), i32),
        vmem((COLS, 8, B), f32),
        vmem((528, B), f32),
        vmem((COLS, PART, B), f32), vmem((COLS, PART, B), f32),
        vmem((ROWS, PART, B), f32), vmem((ROWS, PART, B), f32),
        vmem((FEAT, B), f32), vmem((FEAT, B), f32),
        vmem((ROWS, FEAT, B), f32), vmem((COLS, FEAT, B), f32),
        vmem((COLS, FEAT, B), f32), vmem((COLS, FEAT, B), f32),
        vmem((ROWS, FEAT, B), f32), vmem((ROWS, FEAT, B), f32),
        dma((8,)),
    ]
    for count in (ROWS, COLS, COLS, ROWS, ROWS, COLS, COLS, ROWS):
        scratch += [dma((count,)), dma((count,))]
    return pl.pallas_call(
        kernel,
        out_shape=jax.ShapeDtypeStruct((FEAT, B), f32),
        in_specs=[pl.BlockSpec(memory_space=pl.ANY)] * 8,
        out_specs=pl.BlockSpec(memory_space=pltpu.VMEM),
        scratch_shapes=scratch,
        compiler_params=pltpu.CompilerParams(
            collective_id=0, has_side_effects=True, vmem_limit_bytes=48 * 1024 * 1024
        ),
        name="graph_layer",
    )(*args)


def solution(mesh):
    placed = (
        P(None, ("row", "col")),
        P(None, ("row", "col")),
        P(None, ("row", "col")),
        P(),
        P(),
        P(None, "row"),
        P(),
        P(),
    )
    return jax.shard_map(
        per_device, mesh=mesh, in_specs=placed, out_specs=P(None, ("row", "col")), check_vma=False
    )
```

```python
import jax
import jax.numpy as jnp
from jax import lax
from jax.experimental import pallas as pl
from jax.experimental.pallas import tpu as pltpu
from jax.sharding import PartitionSpec as P

KEEP = 0.05
GO = 1.0 - KEEP
HIGHEST = lax.Precision.HIGHEST
MESH = pl.DeviceIdType.MESH
f32, bf16, i32 = jnp.float32, jnp.bfloat16, jnp.int32

ROWS = 8
COLS = 16
B = 256
SLOTS = 3
EMB = 40
FEAT = 32
ALL = 2 * EMB + FEAT
HALF1 = 8
HALF2 = 8
PART = FEAT + 8


def halves(x):
    hi = x.astype(bf16).astype(f32)
    return hi, x - hi


def transposed_dot(a, b):
    return lax.dot_general(
        a, b, (((0,), (0,)), ((), ())), precision=HIGHEST, preferred_element_type=f32
    )


def kernel(
    emb_first, emb_second, signal, theta_first, theta_second, neighbors, w_forward, w_backward,
    out,
    emb1, emb2, theta1, theta2, near, wf, wb,
    rows, cols, right, left, xs, st, hot, idx, weight, acc,
    f_part, f_got, b_part, b_got, f_home, colx, rowx, f_part2, f_got2, b_part2, b_got2,
    in_sem, cm_send, cm_recv, cs_send, cs_recv, rm_send, rm_recv, rs_send, rs_recv,
    f_send, f_recv, b_send, b_recv, c2_send, c2_recv, r2_send, r2_recv,
    f2_send, f2_recv, b2_send, b2_recv,
):
    r = lax.axis_index("row")
    c = lax.axis_index("col")
    half = c // ROWS
    q = c % ROWS
    base = c - q
    z, x_lo = r // 2, r % 2
    maker = (z + 2 * (c % 2) + (c // 2) % 2) % 4 * 2 + (x_lo + (c // 4) % 2) % 2
    block_start = (2 * maker + half) * (ROWS * B)
    same = q == 0

    def user(k):
        away = (z + 4 - k // 2) % 4
        return base + 4 * ((x_lo + k) % 2) + 2 * (away % 2) + away // 2

    others = jnp.where(same, 0, 1).astype(i32)

    barrier = pltpu.get_barrier_semaphore()

    def greet(i, carry):
        pl.semaphore_signal(barrier, inc=1, device_id=(r, (c + i) % COLS), device_id_type=MESH)
        return carry

    def greet_columns(k, carry):
        @pl.when(jnp.logical_not(jnp.logical_and(same, k == r)))
        def _():
            pl.semaphore_signal(barrier, inc=1, device_id=(k, user(k)), device_id_type=MESH)

        @pl.when(jnp.logical_not(jnp.logical_and(same, k == q)))
        def _():
            pl.semaphore_signal(barrier, inc=1, device_id=(maker, base + k), device_id_type=MESH)

        return carry

    lax.fori_loop(1, COLS, greet, 0)
    lax.fori_loop(0, ROWS, greet_columns, 0)

    fetches = [
        pltpu.make_async_copy(src, dst, in_sem.at[n])
        for n, (src, dst) in enumerate(
            [
                (emb_first, emb1), (emb_second, emb2), (theta_first, theta1),
                (theta_second, theta2), (signal, rows.at[c, pl.ds(2 * EMB, FEAT)]),
                (neighbors, near), (w_forward, wf), (w_backward, wb),
            ]
        )
    ]
    for fetch in fetches:
        fetch.start()
    for fetch in fetches[:5]:
        fetch.wait()
    rows[c, 0:EMB, :] = jnp.tanh(3.0 * transposed_dot(theta1[...], emb1[...]))
    rows[c, EMB : 2 * EMB, :] = jnp.tanh(3.0 * transposed_dot(theta2[...], emb2[...]))

    pl.semaphore_wait(barrier, COLS - 1 + 2 * (ROWS - 1) + 2 * others)

    def to_users(k, src, dst, send, recv):
        return pltpu.make_async_remote_copy(
            src_ref=src, dst_ref=dst.at[q], send_sem=send.at[k], recv_sem=recv.at[q],
            device_id=(k, user(k)), device_id_type=MESH,
        )

    def to_row(k, src, dst, send, recv):
        return pltpu.make_async_remote_copy(
            src_ref=src, dst_ref=dst.at[c], send_sem=send.at[k], recv_sem=recv.at[c],
            device_id=(r, k), device_id_type=MESH,
        )

    def to_homes(k, src, dst, send, recv):
        return pltpu.make_async_remote_copy(
            src_ref=src, dst_ref=dst.at[r], send_sem=send.at[k], recv_sem=recv.at[r],
            device_id=(maker, base + k), device_id_type=MESH,
        )

    def arrival(dst, slot, send, recv):
        return pltpu.make_async_remote_copy(
            src_ref=dst.at[slot], dst_ref=dst.at[slot], send_sem=send.at[slot],
            recv_sem=recv.at[slot], device_id=(r, (c + 1) % COLS), device_id_type=MESH,
        )

    def twin(k):
        return k + 1 - 2 * (k % 2)

    def across(k):
        return k + 2 - 4 * ((k // 2) % 2)

    def around(k, n):
        return (k + 4 * n) % COLS

    def order(t):
        i = t // 2
        k = i // 2
        slot = around(c, k + (k // 2) * (1 - 2 * (k % 2)))
        slot = slot + (i % 2) * (2 - 4 * ((slot // 2) % 2))
        return slot + (t % 2) * (1 - 2 * (slot % 2))

    M = pl.ds(0, 2 * EMB)
    S = pl.ds(2 * EMB, FEAT)

    def pass_on(to, src_buf, slot, dst_buf, part, n, send, recv):
        return pltpu.make_async_remote_copy(
            src_ref=src_buf.at[slot, part], dst_ref=dst_buf.at[slot, part],
            send_sem=send.at[n], recv_sem=recv.at[slot],
            device_id=(r, to), device_id_type=MESH,
        )

    def row_arrival(buf, slot, part, send, recv):
        return pltpu.make_async_remote_copy(
            src_ref=buf.at[slot, part], dst_ref=buf.at[slot, part], send_sem=send.at[0],
            recv_sem=recv.at[slot], device_id=(r, twin(c)), device_id_type=MESH,
        )

    def users_each(do):
        def step(i, carry):
            k = (r + i) % ROWS

            @pl.when(jnp.logical_not(jnp.logical_and(same, k == r)))
            def _():
                do(k)

            return carry

        lax.fori_loop(0, ROWS, step, 0)

    def home_to(k, part, send, recv):
        return pltpu.make_async_remote_copy(
            src_ref=rows.at[c, part], dst_ref=cols.at[q, part], send_sem=send.at[k],
            recv_sem=recv.at[q], device_id=(k, user(k)), device_id_type=MESH,
        )

    def homes_arrived(buf, part, send, recv):
        def step(k, carry):
            @pl.when(jnp.logical_not(jnp.logical_and(same, k == q)))
            def _():
                pltpu.make_async_remote_copy(
                    src_ref=buf.at[k, part], dst_ref=buf.at[k, part], send_sem=send.at[k],
                    recv_sem=recv.at[k], device_id=(r, twin(c)), device_id_type=MESH,
                ).wait_recv()

            return carry

        lax.fori_loop(0, ROWS, step, 0)

    def share_with_users(src, dst, send, recv):
        users_each(lambda k: to_users(k, src, dst, send, recv).start())

        @pl.when(same)
        def _():
            dst[q] = src[...]

    def row_copies(buf, part, send, recv):
        far = [around(c, 1), around(c, 3), around(c, 2)]
        make = lambda to, slot, n: pass_on(to, buf, slot, buf, part, n, send, recv)
        mine = [make(across(c), c, 0)] + [make(to, c, 1 + n) for n, to in enumerate(far)]
        mine += [make(twin(c), c, 4)]
        relayed = [make(to, across(c), 5 + n) for n, to in enumerate(far)]
        relayed += [make(twin(c), across(c), 8)]
        return mine, relayed

    def to_twin(i, buf, part, send, recv):
        return pass_on(twin(c), buf, order(2 * i), buf, part, 7 + i, send, recv)

    m_mine, m_relayed = row_copies(rows, M, rm_send, rm_recv)
    s_mine, s_relayed = row_copies(rows, S, rs_send, rs_recv)
    m_mine[0].start()
    users_each(lambda k: home_to(k, M, cm_send, cm_recv).start())
    for copy in m_mine[1:]:
        copy.start()
    s_mine[0].start()
    users_each(lambda k: home_to(k, S, cs_send, cs_recv).start())
    for copy in s_mine[1:]:
        copy.start()

    @pl.when(same)
    def _():
        cols[q] = rows[c]

    fetches[5].wait()

    def find(g, carry):
        span = pl.ds(pl.multiple_of(g * B, B), B)
        local = near[:, span] - block_start
        slot = [jnp.full((1, B), -1, i32) for _ in range(SLOTS)]
        for k in range(near.shape[0]):
            entry = local[k : k + 1]
            inside = jnp.logical_and(entry >= 0, entry < ROWS * B)
            slot = [
                jnp.where(inside, entry, slot[0]),
                jnp.where(inside, slot[0], slot[1]),
                jnp.where(inside, slot[1], slot[2]),
            ]
        place = lax.broadcasted_iota(i32, (B, B), 0)
        for j in range(SLOTS):
            hot[g, :, j * B : (j + 1) * B] = (place == (slot[j] & (B - 1))).astype(f32).astype(bf16)
        idx[g] = jnp.concatenate(slot + [jnp.full((8 - SLOTS, B), -1, i32)], axis=0)
        return carry

    lax.fori_loop(0, COLS, find, 0)

    def put_columns(values, v):
        hi, lo = halves(values)
        xs[v * 64 : v * 64 + 64, :] = jnp.concatenate([hi, lo], axis=0).astype(bf16)

    row_arrival(rows, across(c), M, rm_send, rm_recv).wait_recv()
    for copy in m_relayed:
        copy.start()
    homes_arrived(cols, M, cm_send, cm_recv)
    for v in range(ROWS):
        turned = jnp.concatenate([cols[v, EMB : 2 * EMB, :], -cols[v, 0:EMB, :]], axis=0)
        hi, lo = halves(turned)
        right[v * B : (v + 1) * B, :] = jnp.concatenate([hi, hi, lo], axis=0).T.astype(bf16)

    def forward(g):
        picked = jnp.dot(xs[...], hot[g], preferred_element_type=f32)
        total = jnp.zeros((FEAT, B), f32)
        for j in range(SLOTS):
            window = idx[g, j : j + 1, :] >> 8
            part = jnp.zeros((2 * FEAT, B), f32)
            for v in range(ROWS):
                part = jnp.where(
                    window == v, picked[v * 64 : v * 64 + 64, j * B : (j + 1) * B], part
                )
            total = total + weight[g, j : j + 1, :] * (part[:FEAT] + part[FEAT:])
        return total

    def score_step(t, carry):
        g = order(t)

        @pl.when(jnp.logical_or(t % 2 == 1, t >= 4))
        def _():
            row_arrival(rows, g, M, rm_send, rm_recv).wait_recv()

        @pl.when(jnp.logical_and(t % 2 == 0, t >= 4))
        def _():
            to_twin(t // 2, rows, M, rm_send, rm_recv).start()

        @pl.when(t == 4)
        def _():
            row_arrival(rows, across(c), S, rs_send, rs_recv).wait_recv()
            for copy in s_relayed:
                copy.start()

        hi, lo = halves(rows[g, 0 : 2 * EMB, :])
        left[...] = jnp.concatenate([hi, lo, hi], axis=0).astype(bf16)
        eight = lax.broadcasted_iota(i32, (8, B), 0)
        gap = [idx[g, j : j + 1, :] - eight for j in range(SLOTS)]
        found = [jnp.zeros((8, B), f32) for _ in range(SLOTS)]
        for v in range(ROWS):
            score = jnp.dot(
                right[v * B : (v + 1) * B, :], left[...], preferred_element_type=f32
            )
            for t in range(B // 8):
                for j in range(SLOTS):
                    found[j] = jnp.where(
                        gap[j] == v * B + 8 * t, score[8 * t : 8 * t + 8], found[j]
                    )
        sums = jnp.zeros((1, B), f32)
        for j in range(SLOTS):
            value = jnp.tanh(3.0 * jnp.sum(found[j], axis=0, keepdims=True))
            value = jnp.where(idx[g, j : j + 1, :] >= 0, jnp.maximum(value, 0.0), 0.0)
            weight[g, j : j + 1, :] = value
            sums = sums + value
        f_part[g, FEAT:PART, :] = jnp.broadcast_to(sums, (8, B))
        return carry

    lax.fori_loop(0, COLS, score_step, 0)
    homes_arrived(cols, S, cs_send, cs_recv)
    for v in range(ROWS):
        put_columns(cols[v, 2 * EMB : ALL, :], v)

    def first_step(t, carry):
        g = order((t + 1) % COLS)

        @pl.when(jnp.logical_and(t % 2 == 0, t >= 4))
        def _():
            row_arrival(rows, order(t), S, rs_send, rs_recv).wait_recv()
            to_twin(t // 2, rows, S, rs_send, rs_recv).start()

        f_part[g, 0:FEAT, :] = forward(g)

        @pl.when(t < COLS - 1)
        def _():
            to_row(g, f_part.at[g], f_got, f_send, f_recv).start()

        return carry

    lax.fori_loop(0, COLS, first_step, 0)

    def backward(first, last, rows_of, ready, with_degree):
        if first == 0:
            acc[...] = jnp.zeros_like(acc)

        def step(t, carry):
            g = order(t)
            ready(t, g)
            x = rows_of(g)
            for j in range(SLOTS):
                window = idx[g, j : j + 1, :] >> 8
                value = weight[g, j : j + 1, :]
                hi, lo = halves(x * value)
                both = jnp.concatenate([hi, lo], axis=0)
                for v in range(ROWS):
                    st[v * 64 : v * 64 + 64, j * B : (j + 1) * B] = jnp.where(
                        window == v, both, 0.0
                    ).astype(bf16)
                if with_degree:
                    hi, lo = halves(value)
                    mine = lax.broadcasted_iota(i32, (8, B), 0) == window
                    st[512:528, j * B : (j + 1) * B] = jnp.concatenate(
                        [jnp.where(mine, hi, 0.0), jnp.where(mine, lo, 0.0)], axis=0
                    ).astype(bf16)
            depth = 528 if with_degree else 512
            acc[0:depth, :] += lax.dot_general(
                st[0:depth, :], hot[g], (((1,), (1,)), ((), ())), preferred_element_type=f32
            )
            return carry

        lax.fori_loop(first, last, step, 0)

    def keep_backward(part, with_degree):
        for v in range(ROWS):
            part[v, 0:FEAT, :] = acc[v * 64 : v * 64 + 32, :] + acc[v * 64 + 32 : v * 64 + 64, :]
            if with_degree:
                part[v, FEAT:PART, :] = jnp.broadcast_to(
                    acc[512 + v : 513 + v, :] + acc[520 + v : 521 + v, :], (8, B)
                )

    def give_back(part, got, send, recv):
        def step(k, carry):
            @pl.when(jnp.logical_not(jnp.logical_and(same, k == q)))
            def _():
                to_homes(k, part.at[k], got, send, recv).start()

            return carry

        lax.fori_loop(0, ROWS, step, 0)

        @pl.when(same)
        def _():
            got[r] = part[q]

    def add_forward(part, got, send, recv):
        def step(i, total):
            k = (c + COLS - i) % COLS
            arrival(got, k, send, recv).wait_recv()
            return total + got[k]

        return lax.fori_loop(1, COLS, step, part[c])

    def add_backward(got, send, recv):
        def step(k, total):
            @pl.when(jnp.logical_not(jnp.logical_and(same, k == r)))
            def _():
                arrival(got, k, send, recv).wait_recv()

            return total + got[k]

        return lax.fori_loop(0, ROWS, step, jnp.zeros(got.shape[1:], f32))

    def signal_ready(t, g):
        @pl.when(t % 2 == 1)
        def _():
            row_arrival(rows, g, S, rs_send, rs_recv).wait_recv()

    own_signal = lambda g: rows[g, 2 * EMB : ALL, :]
    backward(0, HALF1, own_signal, signal_ready, True)

    own = rows[c, 2 * EMB : ALL, :]
    summed = add_forward(f_part, f_got, f_send, f_recv)
    f_scale = GO / (1.0 + summed[FEAT : FEAT + 1])
    f_home[...] = KEEP * own + (summed[:FEAT] + own) * f_scale
    share_with_users(f_home, colx, c2_send, c2_recv)

    backward(HALF1, COLS, own_signal, signal_ready, True)
    keep_backward(b_part, True)
    give_back(b_part, b_got, b_send, b_recv)

    homes_arrived(colx, pl.ds(0, FEAT), c2_send, c2_recv)
    for v in range(ROWS):
        put_columns(colx[v], v)

    def second_step(t, carry):
        g = order(t + 1)
        f_part2[g] = forward(g)
        to_row(g, f_part2.at[g], f_got2, f2_send, f2_recv).start()
        return carry

    lax.fori_loop(0, HALF2, second_step, 0)

    summed = add_backward(b_got, b_send, b_recv)
    b_scale = GO / (1.0 + summed[FEAT : FEAT + 1])
    rowx[c] = KEEP * own + (summed[:FEAT] + own) * b_scale
    A = pl.ds(0, FEAT)
    x_mine, x_relayed = row_copies(rowx, A, r2_send, r2_recv)
    for copy in x_mine:
        copy.start()

    def relay(t):
        @pl.when(t == HALF2 + 2)
        def _():
            row_arrival(rowx, across(c), A, r2_send, r2_recv).wait_recv()
            for copy in x_relayed:
                copy.start()

    def second_late(t, carry):
        relay(t)
        return second_step(t, carry)

    lax.fori_loop(HALF2, COLS - 1, second_late, 0)
    f_part2[c] = forward(c)

    def ready(t, g):
        @pl.when(jnp.logical_or(t % 2 == 1, t >= 4))
        def _():
            row_arrival(rowx, g, A, r2_send, r2_recv).wait_recv()

        @pl.when(jnp.logical_and(t % 2 == 0, t >= 4))
        def _():
            to_twin(t // 2, rowx, A, r2_send, r2_recv).start()

    backward(0, COLS, lambda g: rowx[g], ready, False)
    keep_backward(b_part2, False)
    give_back(b_part2, b_got2, b2_send, b2_recv)

    fetches[6].wait()
    fetches[7].wait()
    first = f_home[...]
    summed = add_forward(f_part2, f_got2, f2_send, f2_recv)
    second = KEEP * own + (summed + first) * f_scale
    mixed = transposed_dot(wf[...], jnp.concatenate([own, first, second], axis=0))
    first = rowx[c]
    summed = add_backward(b_got2, b2_send, b2_recv)
    second = KEEP * own + (summed + first) * b_scale
    out[...] = mixed + transposed_dot(wb[...], jnp.concatenate([own, first, second], axis=0))

    def sent(k):
        home_to(k, M, cm_send, cm_recv).wait_send()
        home_to(k, S, cs_send, cs_recv).wait_send()
        to_users(k, f_home, colx, c2_send, c2_recv).wait_send()

    users_each(sent)

    def sent_to_homes(k, carry):
        @pl.when(jnp.logical_not(jnp.logical_and(same, k == q)))
        def _():
            to_homes(k, b_part.at[k], b_got, b_send, b_recv).wait_send()
            to_homes(k, b_part2.at[k], b_got2, b2_send, b2_recv).wait_send()

        return carry

    def sent_to_row(i, carry):
        k = (c + i) % COLS
        to_row(k, f_part.at[k], f_got, f_send, f_recv).wait_send()
        to_row(k, f_part2.at[k], f_got2, f2_send, f2_recv).wait_send()
        return carry

    lax.fori_loop(0, ROWS, sent_to_homes, 0)
    lax.fori_loop(1, COLS, sent_to_row, 0)
    for copy in m_mine + m_relayed + s_mine + s_relayed + x_mine + x_relayed:
        copy.wait_send()

    def sent_to_twin(i, carry):
        to_twin(i, rows, M, rm_send, rm_recv).wait_send()
        to_twin(i, rows, S, rs_send, rs_recv).wait_send()
        to_twin(i, rowx, A, r2_send, r2_recv).wait_send()
        return carry

    lax.fori_loop(2, ROWS, sent_to_twin, 0)


def per_device(*args):
    vmem = pltpu.VMEM
    keep_count = args[5].shape[0]
    dma = pltpu.SemaphoreType.DMA
    scratch = [
        vmem((EMB, B), f32), vmem((EMB, B), f32), vmem((EMB, EMB), f32), vmem((EMB, EMB), f32),
        vmem((keep_count, COLS * B), i32), vmem((3 * FEAT, FEAT), f32), vmem((3 * FEAT, FEAT), f32),
        vmem((COLS, ALL, B), f32),
        vmem((ROWS, ALL, B), f32),
        vmem((ROWS * B, 6 * EMB), bf16),
        vmem((6 * EMB, B), bf16),
        vmem((512, B), bf16),
        vmem((528, SLOTS * B), bf16),
        vmem((COLS, B, SLOTS * B), bf16),
        vmem((COLS, 8, B), i32),
        vmem((COLS, 8, B), f32),
        vmem((528, B), f32),
        vmem((COLS, PART, B), f32), vmem((COLS, PART, B), f32),
        vmem((ROWS, PART, B), f32), vmem((ROWS, PART, B), f32),
        vmem((FEAT, B), f32),
        vmem((ROWS, FEAT, B), f32), vmem((COLS, FEAT, B), f32),
        vmem((COLS, FEAT, B), f32), vmem((COLS, FEAT, B), f32),
        vmem((ROWS, FEAT, B), f32), vmem((ROWS, FEAT, B), f32),
        dma((8,)),
    ]
    for count in (ROWS, ROWS, COLS, COLS, COLS, ROWS, ROWS, COLS, COLS, ROWS):
        scratch += [dma((count,)), dma((count,))]
    return pl.pallas_call(
        kernel,
        out_shape=jax.ShapeDtypeStruct((FEAT, B), f32),
        in_specs=[pl.BlockSpec(memory_space=pl.ANY)] * 8,
        out_specs=pl.BlockSpec(memory_space=pltpu.VMEM),
        scratch_shapes=scratch,
        compiler_params=pltpu.CompilerParams(
            collective_id=0, has_side_effects=True, vmem_limit_bytes=48 * 1024 * 1024
        ),
        name="graph_layer",
    )(*args)


def solution(mesh):
    placed = (
        P(None, ("row", "col")),
        P(None, ("row", "col")),
        P(None, ("row", "col")),
        P(),
        P(),
        P(None, "row"),
        P(),
        P(),
    )
    return jax.shard_map(
        per_device, mesh=mesh, in_specs=placed, out_specs=P(None, ("row", "col")), check_vma=False
    )
```

```python
import jax
import jax.numpy as jnp
from jax import lax
from jax.experimental import pallas as pl
from jax.experimental.pallas import tpu as pltpu
from jax.sharding import PartitionSpec as P

KEEP = 0.05
GO = 1.0 - KEEP
HIGHEST = lax.Precision.HIGHEST
MESH = pl.DeviceIdType.MESH
f32, bf16, i32 = jnp.float32, jnp.bfloat16, jnp.int32

ROWS = 8
COLS = 16
B = 256
SLOTS = 3
EMB = 40
FEAT = 32
ALL = 2 * EMB + FEAT
VMEM_BYTES = 60 * 1024 * 1024
SPREAD_AT = 8
STEP = 4
PART = FEAT + 8


def halves(x):
    hi = x.astype(bf16).astype(f32)
    return hi, x - hi


def transposed_dot(a, b):
    return lax.dot_general(
        a, b, (((0,), (0,)), ((), ())), precision=HIGHEST, preferred_element_type=f32
    )


def full_dot(a, b):
    return jnp.dot(a, b, precision=HIGHEST, preferred_element_type=f32)


def kernel(
    emb_first, emb_second, signal, theta_first, theta_second, neighbors, w_forward, w_backward,
    out,
    emb1, emb2, theta1, theta2, near, wf, wb,
    rows, cols, levels, right, left, xs, st, hot, idx, weight, acc,
    f_part, f_pair, f_got, b_part, b_got, f_home, colx, rowx, f_part2, f_pair2, f_got2, b_part2, b_got2,
    in_sem, lm_send, lm_recv, ls_send, ls_recv, cm_send, cm_recv, cs_send, cs_recv,
    rm_send, rm_recv, rs_send, rs_recv,
    f_send, f_recv, b_send, b_recv, c2_send, c2_recv, r2_send, r2_recv,
    f2_send, f2_recv, b2_send, b2_recv, p_send, p_recv, p2_send, p2_recv,
):
    r = lax.axis_index("row")
    c = lax.axis_index("col")
    half = c // ROWS
    q = c % ROWS
    base = c - q
    z, x_lo = r // 2, r % 2
    maker = (z + 2 * (c % 2) + (c // 2) % 2) % 4 * 2 + (x_lo + (c // 4) % 2) % 2
    block_start = (2 * maker + half) * (ROWS * B)
    same = q == 0

    def user(k):
        away = (z + 4 - k // 2) % 4
        return base + 4 * ((x_lo + k) % 2) + 2 * (away % 2) + away // 2

    others = jnp.where(same, 0, 1).astype(i32)

    barrier = pltpu.get_barrier_semaphore()

    def greet(i, carry):
        pl.semaphore_signal(barrier, inc=1, device_id=(r, (c + i) % COLS), device_id_type=MESH)
        return carry

    def greet_columns(k, carry):
        @pl.when(jnp.logical_not(jnp.logical_and(same, k == r)))
        def _():
            pl.semaphore_signal(barrier, inc=1, device_id=(k, user(k)), device_id_type=MESH)

        @pl.when(jnp.logical_not(jnp.logical_and(same, k == q)))
        def _():
            pl.semaphore_signal(barrier, inc=1, device_id=(maker, base + k), device_id_type=MESH)

        return carry

    lax.fori_loop(1, COLS, greet, 0)
    for n in range(1, 4):
        pl.semaphore_signal(
            barrier, inc=1, device_id=((z + n) % 4 * 2 + x_lo, c), device_id_type=MESH
        )

    @pl.when((c // 4) % 2 == 1)
    def _():
        for n in range(4):
            pl.semaphore_signal(
                barrier, inc=1, device_id=(2 * z + 1 - x_lo, c - c % 4 + n), device_id_type=MESH
            )

    lax.fori_loop(0, ROWS, greet_columns, 0)

    fetches = [
        pltpu.make_async_copy(src, dst, in_sem.at[n])
        for n, (src, dst) in enumerate(
            [
                (emb_first, emb1), (emb_second, emb2), (theta_first, theta1),
                (theta_second, theta2), (signal, rows.at[c, pl.ds(2 * EMB, FEAT)]),
                (neighbors, near), (w_forward, wf), (w_backward, wb),
            ]
        )
    ]
    for fetch in fetches:
        fetch.start()
    for fetch in fetches[:5]:
        fetch.wait()
    rows[c, 0:EMB, :] = jnp.tanh(3.0 * transposed_dot(theta1[...], emb1[...]))
    rows[c, EMB : 2 * EMB, :] = jnp.tanh(3.0 * transposed_dot(theta2[...], emb2[...]))

    pl.semaphore_wait(barrier, COLS - 1 + 2 * (ROWS - 1) + 2 * others + 3 + 4 * ((c // 4) % 2))

    def to_users(k, src, dst, send, recv):
        return pltpu.make_async_remote_copy(
            src_ref=src, dst_ref=dst.at[q], send_sem=send.at[k], recv_sem=recv.at[q],
            device_id=(k, user(k)), device_id_type=MESH,
        )

    def to_row(k, src, dst, send, recv):
        return pltpu.make_async_remote_copy(
            src_ref=src, dst_ref=dst.at[c], send_sem=send.at[k], recv_sem=recv.at[c],
            device_id=(r, k), device_id_type=MESH,
        )

    def to_homes(k, src, dst, send, recv):
        return pltpu.make_async_remote_copy(
            src_ref=src, dst_ref=dst.at[r], send_sem=send.at[k], recv_sem=recv.at[r],
            device_id=(maker, base + k), device_id_type=MESH,
        )

    def arrival(dst, slot, send, recv):
        return pltpu.make_async_remote_copy(
            src_ref=dst.at[slot], dst_ref=dst.at[slot], send_sem=send.at[slot],
            recv_sem=recv.at[slot], device_id=(r, (c + 1) % COLS), device_id_type=MESH,
        )

    def twin(k):
        return k + 1 - 2 * (k % 2)

    def across(k):
        return k + 2 - 4 * ((k // 2) % 2)

    def around(k, n):
        return (k + 4 * n) % COLS

    def order(t):
        i = t // 2
        k = i // 2
        slot = around(c, k + (k // 2) * (1 - 2 * (k % 2)))
        slot = slot + (i % 2) * (2 - 4 * ((slot // 2) % 2))
        return slot + (t % 2) * (1 - 2 * (slot % 2))

    M = pl.ds(0, 2 * EMB)
    S = pl.ds(2 * EMB, FEAT)

    def pass_on(to, src_buf, slot, dst_buf, part, n, send, recv):
        return pltpu.make_async_remote_copy(
            src_ref=src_buf.at[slot, part], dst_ref=dst_buf.at[slot, part],
            send_sem=send.at[n], recv_sem=recv.at[slot],
            device_id=(r, to), device_id_type=MESH,
        )

    def row_arrival(buf, slot, part, send, recv):
        return pltpu.make_async_remote_copy(
            src_ref=buf.at[slot, part], dst_ref=buf.at[slot, part], send_sem=send.at[0],
            recv_sem=recv.at[slot], device_id=(r, twin(c)), device_id_type=MESH,
        )

    def users_each(do):
        def step(i, carry):
            k = (r + i) % ROWS

            @pl.when(jnp.logical_not(jnp.logical_and(same, k == r)))
            def _():
                do(k)

            return carry

        lax.fori_loop(0, ROWS, step, 0)

    y_low = (c // 4) % 2
    partner = c + 4 - 8 * y_low
    near_row = (x_lo + y_low) % 2

    def to_level(n, part, send, recv):
        slot = c if n < 3 else partner
        return pltpu.make_async_remote_copy(
            src_ref=rows.at[slot, part], dst_ref=levels.at[n, part], send_sem=send.at[n],
            recv_sem=recv.at[n], device_id=((z + 3 - n % 3) % 4 * 2 + x_lo, c),
            device_id_type=MESH,
        )

    def at_level(n, part, send, recv):
        return pltpu.make_async_remote_copy(
            src_ref=levels.at[n, part], dst_ref=levels.at[n, part], send_sem=send.at[n],
            recv_sem=recv.at[n], device_id=(r, twin(c)), device_id_type=MESH,
        )

    def to_user(n, part, send, recv):
        away = n % 4
        slot = (c if n < 4 else partner) % ROWS
        block = (c if n < 4 else partner)
        src = rows.at[block, part] if away == 0 else levels.at[away - 1 + 3 * (n // 4), part]
        there = base + 4 * y_low + 2 * (away % 2) + away // 2
        mine = jnp.logical_and(y_low == 0, there == c)
        copy = pltpu.make_async_remote_copy(
            src_ref=src, dst_ref=cols.at[slot, part], send_sem=send.at[n],
            recv_sem=recv.at[slot], device_id=(2 * z + near_row, there), device_id_type=MESH,
        )
        return mine, src, slot, copy

    def pass_to_user(n, part, send, recv):
        mine, src, slot, copy = to_user(n, part, send, recv)

        @pl.when(jnp.logical_not(mine))
        def _():
            copy.start()

        @pl.when(mine)
        def _():
            cols[slot, part] = src[...]

    def passed_to_user(n, part, send, recv):
        mine, src, slot, copy = to_user(n, part, send, recv)

        @pl.when(jnp.logical_not(mine))
        def _():
            copy.wait_send()

    def spread(n0, part, l_send, l_recv, send, recv):
        for away in (0, 1, 3, 2):
            if away:
                at_level(away - 1 + 3 * n0, part, l_send, l_recv).wait_recv()
            pass_to_user(away + 4 * n0, part, send, recv)

    def homes_arrived(buf, part, send, recv, kept):
        def step(k, carry):
            @pl.when(jnp.logical_not(kept(k)))
            def _():
                pltpu.make_async_remote_copy(
                    src_ref=buf.at[k, part], dst_ref=buf.at[k, part], send_sem=send.at[k],
                    recv_sem=recv.at[k], device_id=(r, twin(c)), device_id_type=MESH,
                ).wait_recv()

            return carry

        lax.fori_loop(0, ROWS, step, 0)

    def share_with_users(src, dst, send, recv):
        users_each(lambda k: to_users(k, src, dst, send, recv).start())

        @pl.when(same)
        def _():
            dst[q] = src[...]

    def row_copies(buf, part, send, recv):
        far = [around(c, 1), around(c, 3), around(c, 2)]
        make = lambda to, slot, n: pass_on(to, buf, slot, buf, part, n, send, recv)
        mine = [make(across(c), c, 0)] + [make(to, c, 1 + n) for n, to in enumerate(far)]
        mine += [make(twin(c), c, 4)]
        relayed = [make(to, across(c), 5 + n) for n, to in enumerate(far)]
        relayed += [make(twin(c), across(c), 8)]
        return mine, relayed

    def to_twin(i, buf, part, send, recv):
        return pass_on(twin(c), buf, order(2 * i), buf, part, 7 + i, send, recv)

    m_mine, m_relayed = row_copies(rows, M, rm_send, rm_recv)
    s_mine, s_relayed = row_copies(rows, S, rs_send, rs_recv)
    for copy in m_mine:
        copy.start()
    for n in range(3):
        to_level(n, M, lm_send, lm_recv).start()
    row_arrival(rows, partner, M, rm_send, rm_recv).wait_recv()
    for n in range(3, 6):
        to_level(n, M, lm_send, lm_recv).start()
    row_arrival(rows, across(c), M, rm_send, rm_recv).wait_recv()
    for copy in m_relayed:
        copy.start()
    spread(0, M, lm_send, lm_recv, cm_send, cm_recv)
    spread(1, M, lm_send, lm_recv, cm_send, cm_recv)
    for copy in s_mine:
        copy.start()
    for n in range(3):
        to_level(n, S, ls_send, ls_recv).start()

    fetches[5].wait()

    def find(g, carry):
        span = pl.ds(pl.multiple_of(g * B, B), B)
        local = near[:, span] - block_start
        slot = [jnp.full((1, B), -1, i32) for _ in range(SLOTS)]
        for k in range(near.shape[0]):
            entry = local[k : k + 1]
            inside = jnp.logical_and(entry >= 0, entry < ROWS * B)
            slot = [
                jnp.where(inside, entry, slot[0]),
                jnp.where(inside, slot[0], slot[1]),
                jnp.where(inside, slot[1], slot[2]),
            ]
        place = lax.broadcasted_iota(i32, (B, B), 0)
        for j in range(SLOTS):
            hot[g, :, j * B : (j + 1) * B] = (place == (slot[j] & (B - 1))).astype(f32).astype(bf16)
        idx[g] = jnp.concatenate(slot + [jnp.full((8 - SLOTS, B), -1, i32)], axis=0)
        return carry

    lax.fori_loop(0, COLS, find, 0)

    def put_columns(values, v):
        hi, lo = halves(values)
        xs[v * 64 : v * 64 + 64, :] = jnp.concatenate([hi, lo], axis=0).astype(bf16)

    homes_arrived(cols, M, cm_send, cm_recv, lambda k: jnp.logical_and(y_low == 0, k % 4 == q % 4))
    for v in range(ROWS):
        turned = jnp.concatenate([cols[v, EMB : 2 * EMB, :], -cols[v, 0:EMB, :]], axis=0)
        hi, lo = halves(turned)
        right[v * B : (v + 1) * B, :] = jnp.concatenate([hi, hi, lo], axis=0).T.astype(bf16)

    def forward(g):
        picked = jnp.dot(xs[...], hot[g], preferred_element_type=f32)
        total = jnp.zeros((FEAT, B), f32)
        for j in range(SLOTS):
            window = idx[g, j : j + 1, :] >> 8
            part = jnp.zeros((2 * FEAT, B), f32)
            for v in range(ROWS):
                part = jnp.where(
                    window == v, picked[v * 64 : v * 64 + 64, j * B : (j + 1) * B], part
                )
            total = total + weight[g, j : j + 1, :] * (part[:FEAT] + part[FEAT:])
        return total

    def score_step(t, carry):
        g = order(t)

        @pl.when(jnp.logical_or(t % 2 == 1, jnp.logical_and(t >= 4, g != partner)))
        def _():
            row_arrival(rows, g, M, rm_send, rm_recv).wait_recv()

        @pl.when(jnp.logical_and(t % 2 == 0, t >= 4))
        def _():
            to_twin(t // 2, rows, M, rm_send, rm_recv).start()

        @pl.when(t == 4)
        def _():
            row_arrival(rows, partner, S, rs_send, rs_recv).wait_recv()
            for n in range(3, 6):
                to_level(n, S, ls_send, ls_recv).start()
            row_arrival(rows, across(c), S, rs_send, rs_recv).wait_recv()
            for copy in s_relayed:
                copy.start()

        hi, lo = halves(rows[g, 0 : 2 * EMB, :])
        left[...] = jnp.concatenate([hi, lo, hi], axis=0).astype(bf16)
        eight = lax.broadcasted_iota(i32, (8, B), 0)
        gap = [idx[g, j : j + 1, :] - eight for j in range(SLOTS)]
        found = [jnp.zeros((8, B), f32) for _ in range(SLOTS)]
        for v in range(ROWS):
            score = jnp.dot(
                right[v * B : (v + 1) * B, :], left[...], preferred_element_type=f32
            )
            for t in range(B // 8):
                for j in range(SLOTS):
                    found[j] = jnp.where(
                        gap[j] == v * B + 8 * t, score[8 * t : 8 * t + 8], found[j]
                    )
        sums = jnp.zeros((1, B), f32)
        for j in range(SLOTS):
            value = jnp.tanh(3.0 * jnp.sum(found[j], axis=0, keepdims=True))
            value = jnp.where(idx[g, j : j + 1, :] >= 0, jnp.maximum(value, 0.0), 0.0)
            weight[g, j : j + 1, :] = value
            sums = sums + value
        f_part[g, FEAT:PART, :] = jnp.broadcast_to(sums, (8, B))
        return carry

    lax.fori_loop(0, SPREAD_AT, score_step, 0)
    spread(0, S, ls_send, ls_recv, cs_send, cs_recv)
    spread(1, S, ls_send, ls_recv, cs_send, cs_recv)
    lax.fori_loop(SPREAD_AT, COLS, score_step, 0)
    homes_arrived(cols, S, cs_send, cs_recv, lambda k: jnp.logical_and(y_low == 0, k % 4 == q % 4))
    for v in range(ROWS):
        put_columns(cols[v, 2 * EMB : ALL, :], v)

    def pair_sum(g, part, pair, send, recv):
        return pltpu.make_async_remote_copy(
            src_ref=part.at[g], dst_ref=pair.at[g], send_sem=send.at[g], recv_sem=recv.at[g],
            device_id=(r, twin(c)), device_id_type=MESH,
        )

    def forward_hop(part, pair, got, p_send, p_recv, send, recv, before):
        def for_twin(h, carry):
            before(h)
            blocks = [order(2 * (h * STEP + n) + 1) for n in range(STEP)]
            sums = [forward(g) for g in blocks]
            for g, total in zip(blocks, sums):
                part[g, 0:FEAT, :] = total
            for g in blocks:
                pair_sum(g, part, pair, p_send, p_recv).start()
            return carry

        def for_others(h, carry):
            before(h + ROWS // STEP)
            late = [(h * STEP + n + 1) % ROWS for n in range(STEP)]
            blocks = [order(2 * i) for i in late]
            sums = [forward(g) for g in blocks]
            for g, total in zip(blocks, sums):
                part[g, 0:FEAT, :] = total
            for g, i in zip(blocks, late):
                pair_sum(g, part, pair, p_send, p_recv).wait_recv()
                part[g] = part[g] + pair[g]

                @pl.when(i > 0)
                def _():
                    to_row(g, part.at[g], got, send, recv).start()

            return carry

        lax.fori_loop(0, ROWS // STEP, for_twin, 0)
        lax.fori_loop(0, ROWS // STEP, for_others, 0)

    def signals_on(h):
        for n in range(0, STEP, 2):
            t = h * STEP + n

            @pl.when(t >= 4)
            def _():
                @pl.when(order(t) != partner)
                def _():
                    row_arrival(rows, order(t), S, rs_send, rs_recv).wait_recv()

                to_twin(t // 2, rows, S, rs_send, rs_recv).start()

    forward_hop(f_part, f_pair, f_got, p_send, p_recv, f_send, f_recv, signals_on)

    def backward(rows_of, ready, with_degree):
        acc[...] = jnp.zeros_like(acc)
        depth = 528 if with_degree else 512

        def fill(g, n):
            x = rows_of(g)
            for j in range(SLOTS):
                window = idx[g, j : j + 1, :] >> 8
                value = weight[g, j : j + 1, :]
                hi, lo = halves(x * value)
                both = jnp.concatenate([hi, lo], axis=0)
                for v in range(ROWS):
                    st[n, v * 64 : v * 64 + 64, j * B : (j + 1) * B] = jnp.where(
                        window == v, both, 0.0
                    ).astype(bf16)
                if with_degree:
                    hi, lo = halves(value)
                    mine = lax.broadcasted_iota(i32, (8, B), 0) == window
                    st[n, 512:528, j * B : (j + 1) * B] = jnp.concatenate(
                        [jnp.where(mine, hi, 0.0), jnp.where(mine, lo, 0.0)], axis=0
                    ).astype(bf16)

        def step(h, carry):
            blocks = [order(h * STEP + n) for n in range(STEP)]
            for n, g in enumerate(blocks):
                ready(h * STEP + n, g)
            for n, g in enumerate(blocks):
                fill(g, n)
            total = acc[0:depth, :]
            for n, g in enumerate(blocks):
                total = total + lax.dot_general(
                    st[n, 0:depth, :], hot[g], (((1,), (1,)), ((), ())),
                    preferred_element_type=f32,
                )
            acc[0:depth, :] = total
            return carry

        lax.fori_loop(0, COLS // STEP, step, 0)

    def keep_backward(part, with_degree):
        for v in range(ROWS):
            part[v, 0:FEAT, :] = acc[v * 64 : v * 64 + 32, :] + acc[v * 64 + 32 : v * 64 + 64, :]
            if with_degree:
                part[v, FEAT:PART, :] = jnp.broadcast_to(
                    acc[512 + v : 513 + v, :] + acc[520 + v : 521 + v, :], (8, B)
                )

    def give_back(part, got, send, recv):
        def step(k, carry):
            @pl.when(jnp.logical_not(jnp.logical_and(same, k == q)))
            def _():
                to_homes(k, part.at[k], got, send, recv).start()

            return carry

        lax.fori_loop(0, ROWS, step, 0)

        @pl.when(same)
        def _():
            got[r] = part[q]

    def add_forward(part, got, send, recv):
        def step(n, total):
            k = (c + 2 * n) % COLS
            arrival(got, k, send, recv).wait_recv()
            return total + got[k]

        return lax.fori_loop(1, ROWS, step, part[c])

    def add_backward(got, send, recv):
        def step(k, total):
            @pl.when(jnp.logical_not(jnp.logical_and(same, k == r)))
            def _():
                arrival(got, k, send, recv).wait_recv()

            return total + got[k]

        return lax.fori_loop(0, ROWS, step, jnp.zeros(got.shape[1:], f32))

    def signal_ready(t, g):
        @pl.when(t % 2 == 1)
        def _():
            row_arrival(rows, g, S, rs_send, rs_recv).wait_recv()

    own_signal = lambda g: rows[g, 2 * EMB : ALL, :]
    backward(own_signal, signal_ready, True)
    keep_backward(b_part, True)
    give_back(b_part, b_got, b_send, b_recv)

    own = rows[c, 2 * EMB : ALL, :]
    summed = add_forward(f_part, f_got, f_send, f_recv)
    f_scale = GO / (1.0 + summed[FEAT : FEAT + 1])
    f_home[...] = KEEP * own + (summed[:FEAT] + own) * f_scale
    share_with_users(f_home, colx, c2_send, c2_recv)

    summed = add_backward(b_got, b_send, b_recv)
    b_scale = GO / (1.0 + summed[FEAT : FEAT + 1])
    rowx[c] = KEEP * own + (summed[:FEAT] + own) * b_scale
    A = pl.ds(0, FEAT)

    def to_chip(n):
        return pass_on((c + 2 * n) % COLS, rowx, c, rowx, A, n, r2_send, r2_recv)

    def on_to_twin(n):
        return pass_on(twin(c), rowx, (c + 2 * n) % COLS, rowx, A, ROWS + n, r2_send, r2_recv)

    for n in range(1, ROWS):
        to_chip(n).start()
    on_to_twin(0).start()

    homes_arrived(colx, pl.ds(0, FEAT), c2_send, c2_recv, lambda k: jnp.logical_and(same, k == q))
    for v in range(ROWS):
        put_columns(colx[v], v)

    forward_hop(f_part2, f_pair2, f_got2, p2_send, p2_recv, f2_send, f2_recv, lambda h: None)

    for n in range(1, ROWS):
        row_arrival(rowx, (c + 2 * n) % COLS, A, r2_send, r2_recv).wait_recv()
        on_to_twin(n).start()

    def ready(t, g):
        @pl.when(t % 2 == 1)
        def _():
            row_arrival(rowx, g, A, r2_send, r2_recv).wait_recv()

    backward(lambda g: rowx[g], ready, False)
    keep_backward(b_part2, False)
    give_back(b_part2, b_got2, b2_send, b2_recv)

    fetches[6].wait()
    fetches[7].wait()
    first = f_home[...]
    summed = add_forward(f_part2, f_got2, f2_send, f2_recv)
    second = KEEP * own + (summed + first) * f_scale
    mixed = full_dot(wf[...], jnp.concatenate([own, first, second], axis=0))
    first = rowx[c]
    summed = add_backward(b_got2, b2_send, b2_recv)
    second = KEEP * own + (summed + first) * b_scale
    out[...] = mixed + full_dot(wb[...], jnp.concatenate([own, first, second], axis=0))

    users_each(lambda k: to_users(k, f_home, colx, c2_send, c2_recv).wait_send())

    for n in range(6):
        to_level(n, M, lm_send, lm_recv).wait_send()
        to_level(n, S, ls_send, ls_recv).wait_send()
    for n in range(8):
        passed_to_user(n, M, cm_send, cm_recv)
        passed_to_user(n, S, cs_send, cs_recv)

    def sent_to_homes(k, carry):
        @pl.when(jnp.logical_not(jnp.logical_and(same, k == q)))
        def _():
            to_homes(k, b_part.at[k], b_got, b_send, b_recv).wait_send()
            to_homes(k, b_part2.at[k], b_got2, b2_send, b2_recv).wait_send()

        return carry

    def sent_to_row(n, carry):
        k = (c + 2 * n) % COLS
        to_row(k, f_part.at[k], f_got, f_send, f_recv).wait_send()
        to_row(k, f_part2.at[k], f_got2, f2_send, f2_recv).wait_send()
        to_chip(n).wait_send()
        return carry

    def sent_to_pair(n, carry):
        k = (twin(c) + 2 * n) % COLS
        pair_sum(k, f_part, f_pair, p_send, p_recv).wait_send()
        pair_sum(k, f_part2, f_pair2, p2_send, p2_recv).wait_send()
        on_to_twin(n).wait_send()
        return carry

    lax.fori_loop(0, ROWS, sent_to_pair, 0)
    lax.fori_loop(0, ROWS, sent_to_homes, 0)
    lax.fori_loop(1, ROWS, sent_to_row, 0)
    for copy in m_mine + m_relayed + s_mine + s_relayed:
        copy.wait_send()

    def sent_to_twin(i, carry):
        to_twin(i, rows, M, rm_send, rm_recv).wait_send()
        to_twin(i, rows, S, rs_send, rs_recv).wait_send()
        return carry

    lax.fori_loop(2, ROWS, sent_to_twin, 0)


def per_device(*args):
    vmem = pltpu.VMEM
    keep_count = args[5].shape[0]
    dma = pltpu.SemaphoreType.DMA
    scratch = [
        vmem((EMB, B), f32), vmem((EMB, B), f32), vmem((EMB, EMB), f32), vmem((EMB, EMB), f32),
        vmem((keep_count, COLS * B), i32), vmem((FEAT, 3 * FEAT), f32), vmem((FEAT, 3 * FEAT), f32),
        vmem((COLS, ALL, B), f32),
        vmem((ROWS, ALL, B), f32),
        vmem((6, ALL, B), f32),
        vmem((ROWS * B, 6 * EMB), bf16),
        vmem((6 * EMB, B), bf16),
        vmem((512, B), bf16),
        vmem((STEP, 528, SLOTS * B), bf16),
        vmem((COLS, B, SLOTS * B), bf16),
        vmem((COLS, 8, B), i32),
        vmem((COLS, 8, B), f32),
        vmem((528, B), f32),
        vmem((COLS, PART, B), f32), vmem((COLS, PART, B), f32),
        vmem((COLS, PART, B), f32),
        vmem((ROWS, PART, B), f32), vmem((ROWS, PART, B), f32),
        vmem((FEAT, B), f32),
        vmem((ROWS, FEAT, B), f32), vmem((COLS, FEAT, B), f32),
        vmem((COLS, FEAT, B), f32), vmem((COLS, FEAT, B), f32),
        vmem((COLS, FEAT, B), f32),
        vmem((ROWS, FEAT, B), f32), vmem((ROWS, FEAT, B), f32),
        dma((8,)),
    ]
    for count in (6, 6, ROWS, ROWS, COLS, COLS, COLS, ROWS, ROWS, COLS, COLS, ROWS, COLS, COLS):
        scratch += [dma((count,)), dma((count,))]
    return pl.pallas_call(
        kernel,
        out_shape=jax.ShapeDtypeStruct((FEAT, B), f32),
        in_specs=[pl.BlockSpec(memory_space=pl.ANY)] * 8,
        out_specs=pl.BlockSpec(memory_space=pltpu.VMEM),
        scratch_shapes=scratch,
        compiler_params=pltpu.CompilerParams(
            collective_id=0, has_side_effects=True, vmem_limit_bytes=VMEM_BYTES
        ),
        name="graph_layer",
    )(*args[:6], args[6].T, args[7].T)


def solution(mesh):
    placed = (
        P(None, ("row", "col")),
        P(None, ("row", "col")),
        P(None, ("row", "col")),
        P(),
        P(),
        P(None, "row"),
        P(),
        P(),
    )
    return jax.shard_map(
        per_device, mesh=mesh, in_specs=placed, out_specs=P(None, ("row", "col")), check_vma=False
    )
```

```python
import jax
import jax.numpy as jnp
from jax import lax
from jax.experimental import pallas as pl
from jax.experimental.pallas import tpu as pltpu
from jax.sharding import PartitionSpec as P

KEEP = 0.05
GO = 1.0 - KEEP
HIGHEST = lax.Precision.HIGHEST
MESH = pl.DeviceIdType.MESH
f32, bf16, i32 = jnp.float32, jnp.bfloat16, jnp.int32

ROWS = 8
COLS = 16
B = 256
SLOTS = 3
EMB = 40
FEAT = 32
ALL = 2 * EMB + FEAT
VMEM_BYTES = 60 * 1024 * 1024
STEP = 4
PART = FEAT + 8


def halves(x):
    hi = x.astype(bf16).astype(f32)
    return hi, x - hi


def transposed_dot(a, b):
    return lax.dot_general(
        a, b, (((0,), (0,)), ((), ())), precision=HIGHEST, preferred_element_type=f32
    )


def full_dot(a, b):
    return jnp.dot(a, b, precision=HIGHEST, preferred_element_type=f32)


def kernel(
    emb_first, emb_second, signal, theta_first, theta_second, neighbors, w_forward, w_backward,
    out,
    emb1, emb2, theta1, theta2, near, wf, wb,
    rows, cols, right, left, xs, st, hot, idx, weight, acc,
    f_part, f_pair, f_got, b_part, b_got, f_home, colx, rowx, f_part2, f_pair2, f_got2, b_part2, b_got2,
    in_sem, cm_send, cm_recv, cs_send, cs_recv, rm_send, rm_recv, rs_send, rs_recv,
    f_send, f_recv, b_send, b_recv, c2_send, c2_recv, r2_send, r2_recv,
    f2_send, f2_recv, b2_send, b2_recv, p_send, p_recv, p2_send, p2_recv,
):
    r = lax.axis_index("row")
    c = lax.axis_index("col")
    half = c // ROWS
    q = c % ROWS
    base = c - q
    z, x_lo = r // 2, r % 2
    maker = (z + 2 * (c % 2) + (c // 2) % 2) % 4 * 2 + (x_lo + (c // 4) % 2) % 2
    block_start = (2 * maker + half) * (ROWS * B)
    same = q == 0

    def user(k):
        away = (z + 4 - k // 2) % 4
        return base + 4 * ((x_lo + k) % 2) + 2 * (away % 2) + away // 2

    others = jnp.where(same, 0, 1).astype(i32)

    barrier = pltpu.get_barrier_semaphore()

    def greet(i, carry):
        pl.semaphore_signal(barrier, inc=1, device_id=(r, (c + i) % COLS), device_id_type=MESH)
        return carry

    def greet_columns(k, carry):
        @pl.when(jnp.logical_not(jnp.logical_and(same, k == r)))
        def _():
            pl.semaphore_signal(barrier, inc=1, device_id=(k, user(k)), device_id_type=MESH)

        @pl.when(jnp.logical_not(jnp.logical_and(same, k == q)))
        def _():
            pl.semaphore_signal(barrier, inc=1, device_id=(maker, base + k), device_id_type=MESH)

        return carry

    lax.fori_loop(1, COLS, greet, 0)
    lax.fori_loop(0, ROWS, greet_columns, 0)

    fetches = [
        pltpu.make_async_copy(src, dst, in_sem.at[n])
        for n, (src, dst) in enumerate(
            [
                (emb_first, emb1), (emb_second, emb2), (theta_first, theta1),
                (theta_second, theta2), (signal, rows.at[c, pl.ds(2 * EMB, FEAT)]),
                (neighbors, near), (w_forward, wf), (w_backward, wb),
            ]
        )
    ]
    for fetch in fetches:
        fetch.start()
    for fetch in fetches[:5]:
        fetch.wait()
    rows[c, 0:EMB, :] = jnp.tanh(3.0 * transposed_dot(theta1[...], emb1[...]))
    rows[c, EMB : 2 * EMB, :] = jnp.tanh(3.0 * transposed_dot(theta2[...], emb2[...]))

    pl.semaphore_wait(barrier, COLS - 1 + 2 * (ROWS - 1) + 2 * others)

    def to_users(k, src, dst, send, recv):
        return pltpu.make_async_remote_copy(
            src_ref=src, dst_ref=dst.at[q], send_sem=send.at[k], recv_sem=recv.at[q],
            device_id=(k, user(k)), device_id_type=MESH,
        )

    def to_row(k, src, dst, send, recv):
        return pltpu.make_async_remote_copy(
            src_ref=src, dst_ref=dst.at[c], send_sem=send.at[k], recv_sem=recv.at[c],
            device_id=(r, k), device_id_type=MESH,
        )

    def to_homes(k, src, dst, send, recv):
        return pltpu.make_async_remote_copy(
            src_ref=src, dst_ref=dst.at[r], send_sem=send.at[k], recv_sem=recv.at[r],
            device_id=(maker, base + k), device_id_type=MESH,
        )

    def arrival(dst, slot, send, recv):
        return pltpu.make_async_remote_copy(
            src_ref=dst.at[slot], dst_ref=dst.at[slot], send_sem=send.at[slot],
            recv_sem=recv.at[slot], device_id=(r, (c + 1) % COLS), device_id_type=MESH,
        )

    def twin(k):
        return k + 1 - 2 * (k % 2)

    def across(k):
        return k + 2 - 4 * ((k // 2) % 2)

    def around(k, n):
        return (k + 4 * n) % COLS

    def order(t):
        i = t // 2
        k = i // 2
        slot = around(c, k + (k // 2) * (1 - 2 * (k % 2)))
        slot = slot + (i % 2) * (2 - 4 * ((slot // 2) % 2))
        return slot + (t % 2) * (1 - 2 * (slot % 2))

    M = pl.ds(0, 2 * EMB)
    S = pl.ds(2 * EMB, FEAT)

    def pass_on(to, src_buf, slot, dst_buf, part, n, send, recv):
        return pltpu.make_async_remote_copy(
            src_ref=src_buf.at[slot, part], dst_ref=dst_buf.at[slot, part],
            send_sem=send.at[n], recv_sem=recv.at[slot],
            device_id=(r, to), device_id_type=MESH,
        )

    def row_arrival(buf, slot, part, send, recv):
        return pltpu.make_async_remote_copy(
            src_ref=buf.at[slot, part], dst_ref=buf.at[slot, part], send_sem=send.at[0],
            recv_sem=recv.at[slot], device_id=(r, twin(c)), device_id_type=MESH,
        )

    def users_each(do):
        def step(i, carry):
            k = (r + i) % ROWS

            @pl.when(jnp.logical_not(jnp.logical_and(same, k == r)))
            def _():
                do(k)

            return carry

        lax.fori_loop(0, ROWS, step, 0)

    y_low = (c // 4) % 2
    partner = c + 4 - 8 * y_low
    near_row = (x_lo + y_low) % 2

    def home_to(i, slot, part, send, recv):
        k = 2 * i + near_row
        n = i + 4 * (jnp.where(slot == c, 0, 1).astype(i32))
        return pltpu.make_async_remote_copy(
            src_ref=rows.at[slot, part], dst_ref=cols.at[slot % ROWS, part], send_sem=send.at[n],
            recv_sem=recv.at[slot % ROWS], device_id=(k, user(k)), device_id_type=MESH,
        )

    def homes_each(slot, do):
        def step(j, carry):
            i = (z + j) % 4

            @pl.when(jnp.logical_not(own_user(i)))
            def _():
                do(i, slot)

            return carry

        lax.fori_loop(0, 4, step, 0)

    def own_user(i):
        k = 2 * i + near_row
        return jnp.logical_and(k == r, user(k) == c)

    def homes_arrived(buf, part, send, recv, kept):
        def step(k, carry):
            @pl.when(jnp.logical_not(jnp.logical_and(same, kept(k))))
            def _():
                pltpu.make_async_remote_copy(
                    src_ref=buf.at[k, part], dst_ref=buf.at[k, part], send_sem=send.at[k],
                    recv_sem=recv.at[k], device_id=(r, twin(c)), device_id_type=MESH,
                ).wait_recv()

            return carry

        lax.fori_loop(0, ROWS, step, 0)

    def share_with_users(src, dst, send, recv):
        users_each(lambda k: to_users(k, src, dst, send, recv).start())

        @pl.when(same)
        def _():
            dst[q] = src[...]

    def row_copies(buf, part, send, recv):
        far = [around(c, 1), around(c, 3), around(c, 2)]
        make = lambda to, slot, n: pass_on(to, buf, slot, buf, part, n, send, recv)
        mine = [make(across(c), c, 0)] + [make(to, c, 1 + n) for n, to in enumerate(far)]
        mine += [make(twin(c), c, 4)]
        relayed = [make(to, across(c), 5 + n) for n, to in enumerate(far)]
        relayed += [make(twin(c), across(c), 8)]
        return mine, relayed

    def to_twin(i, buf, part, send, recv):
        return pass_on(twin(c), buf, order(2 * i), buf, part, 7 + i, send, recv)

    m_mine, m_relayed = row_copies(rows, M, rm_send, rm_recv)
    s_mine, s_relayed = row_copies(rows, S, rs_send, rs_recv)
    for copy in (m_mine[1], m_mine[2], m_mine[0]):
        copy.start()
    homes_each(c, lambda i, slot: home_to(i, slot, M, cm_send, cm_recv).start())
    for copy in m_mine[3:]:
        copy.start()

    @pl.when(same)
    def _():
        cols[q] = rows[c]

    def partner_block(part, buf_send, buf_recv, send, recv):
        row_arrival(rows, partner, part, buf_send, buf_recv).wait_recv()
        homes_each(partner, lambda i, slot: home_to(i, slot, part, send, recv).start())

        @pl.when(same)
        def _():
            cols[partner % ROWS, part] = rows[partner, part]

    partner_block(M, rm_send, rm_recv, cm_send, cm_recv)
    row_arrival(rows, across(c), M, rm_send, rm_recv).wait_recv()
    for copy in m_relayed:
        copy.start()
    for copy in s_mine:
        copy.start()
    homes_each(c, lambda i, slot: home_to(i, slot, S, cs_send, cs_recv).start())

    fetches[5].wait()

    def find(g, carry):
        span = pl.ds(pl.multiple_of(g * B, B), B)
        local = near[:, span] - block_start
        slot = [jnp.full((1, B), -1, i32) for _ in range(SLOTS)]
        for k in range(near.shape[0]):
            entry = local[k : k + 1]
            inside = jnp.logical_and(entry >= 0, entry < ROWS * B)
            slot = [
                jnp.where(inside, entry, slot[0]),
                jnp.where(inside, slot[0], slot[1]),
                jnp.where(inside, slot[1], slot[2]),
            ]
        place = lax.broadcasted_iota(i32, (B, B), 0)
        for j in range(SLOTS):
            hot[g, :, j * B : (j + 1) * B] = (place == (slot[j] & (B - 1))).astype(f32).astype(bf16)
        idx[g] = jnp.concatenate(slot + [jnp.full((8 - SLOTS, B), -1, i32)], axis=0)
        return carry

    lax.fori_loop(0, COLS, find, 0)

    def put_columns(values, v):
        hi, lo = halves(values)
        xs[v * 64 : v * 64 + 64, :] = jnp.concatenate([hi, lo], axis=0).astype(bf16)

    homes_arrived(cols, M, cm_send, cm_recv, lambda k: k % 4 == 0)
    for v in range(ROWS):
        turned = jnp.concatenate([cols[v, EMB : 2 * EMB, :], -cols[v, 0:EMB, :]], axis=0)
        hi, lo = halves(turned)
        right[v * B : (v + 1) * B, :] = jnp.concatenate([hi, hi, lo], axis=0).T.astype(bf16)

    def forward(g):
        picked = jnp.dot(xs[...], hot[g], preferred_element_type=f32)
        total = jnp.zeros((FEAT, B), f32)
        for j in range(SLOTS):
            window = idx[g, j : j + 1, :] >> 8
            part = jnp.zeros((2 * FEAT, B), f32)
            for v in range(ROWS):
                part = jnp.where(
                    window == v, picked[v * 64 : v * 64 + 64, j * B : (j + 1) * B], part
                )
            total = total + weight[g, j : j + 1, :] * (part[:FEAT] + part[FEAT:])
        return total

    def score_step(t, carry):
        g = order(t)

        @pl.when(jnp.logical_or(t % 2 == 1, jnp.logical_and(t >= 4, g != partner)))
        def _():
            row_arrival(rows, g, M, rm_send, rm_recv).wait_recv()

        @pl.when(jnp.logical_and(t % 2 == 0, t >= 4))
        def _():
            to_twin(t // 2, rows, M, rm_send, rm_recv).start()

        @pl.when(t == 4)
        def _():
            partner_block(S, rs_send, rs_recv, cs_send, cs_recv)
            row_arrival(rows, across(c), S, rs_send, rs_recv).wait_recv()
            for copy in s_relayed:
                copy.start()

        hi, lo = halves(rows[g, 0 : 2 * EMB, :])
        left[...] = jnp.concatenate([hi, lo, hi], axis=0).astype(bf16)
        eight = lax.broadcasted_iota(i32, (8, B), 0)
        gap = [idx[g, j : j + 1, :] - eight for j in range(SLOTS)]
        found = [jnp.zeros((8, B), f32) for _ in range(SLOTS)]
        for v in range(ROWS):
            score = jnp.dot(
                right[v * B : (v + 1) * B, :], left[...], preferred_element_type=f32
            )
            for t in range(B // 8):
                for j in range(SLOTS):
                    found[j] = jnp.where(
                        gap[j] == v * B + 8 * t, score[8 * t : 8 * t + 8], found[j]
                    )
        sums = jnp.zeros((1, B), f32)
        for j in range(SLOTS):
            value = jnp.tanh(3.0 * jnp.sum(found[j], axis=0, keepdims=True))
            value = jnp.where(idx[g, j : j + 1, :] >= 0, jnp.maximum(value, 0.0), 0.0)
            weight[g, j : j + 1, :] = value
            sums = sums + value
        f_part[g, FEAT:PART, :] = jnp.broadcast_to(sums, (8, B))
        return carry

    lax.fori_loop(0, COLS, score_step, 0)
    homes_arrived(cols, S, cs_send, cs_recv, lambda k: k % 4 == 0)
    for v in range(ROWS):
        put_columns(cols[v, 2 * EMB : ALL, :], v)

    def pair_sum(g, part, pair, send, recv):
        return pltpu.make_async_remote_copy(
            src_ref=part.at[g], dst_ref=pair.at[g], send_sem=send.at[g], recv_sem=recv.at[g],
            device_id=(r, twin(c)), device_id_type=MESH,
        )

    def forward_hop(part, pair, got, p_send, p_recv, send, recv, before):
        def for_twin(h, carry):
            before(h)
            blocks = [order(2 * (h * STEP + n) + 1) for n in range(STEP)]
            sums = [forward(g) for g in blocks]
            for g, total in zip(blocks, sums):
                part[g, 0:FEAT, :] = total
            for g in blocks:
                pair_sum(g, part, pair, p_send, p_recv).start()
            return carry

        def for_others(h, carry):
            before(h + ROWS // STEP)
            late = [(h * STEP + n + 1) % ROWS for n in range(STEP)]
            blocks = [order(2 * i) for i in late]
            sums = [forward(g) for g in blocks]
            for g, total in zip(blocks, sums):
                part[g, 0:FEAT, :] = total
            for g, i in zip(blocks, late):
                pair_sum(g, part, pair, p_send, p_recv).wait_recv()
                part[g] = part[g] + pair[g]

                @pl.when(i > 0)
                def _():
                    to_row(g, part.at[g], got, send, recv).start()

            return carry

        lax.fori_loop(0, ROWS // STEP, for_twin, 0)
        lax.fori_loop(0, ROWS // STEP, for_others, 0)

    def signals_on(h):
        for n in range(0, STEP, 2):
            t = h * STEP + n

            @pl.when(t >= 4)
            def _():
                @pl.when(order(t) != partner)
                def _():
                    row_arrival(rows, order(t), S, rs_send, rs_recv).wait_recv()

                to_twin(t // 2, rows, S, rs_send, rs_recv).start()

    forward_hop(f_part, f_pair, f_got, p_send, p_recv, f_send, f_recv, signals_on)

    def backward(rows_of, ready, with_degree):
        acc[...] = jnp.zeros_like(acc)
        depth = 528 if with_degree else 512

        def fill(g, n):
            x = rows_of(g)
            for j in range(SLOTS):
                window = idx[g, j : j + 1, :] >> 8
                value = weight[g, j : j + 1, :]
                hi, lo = halves(x * value)
                both = jnp.concatenate([hi, lo], axis=0)
                for v in range(ROWS):
                    st[n, v * 64 : v * 64 + 64, j * B : (j + 1) * B] = jnp.where(
                        window == v, both, 0.0
                    ).astype(bf16)
                if with_degree:
                    hi, lo = halves(value)
                    mine = lax.broadcasted_iota(i32, (8, B), 0) == window
                    st[n, 512:528, j * B : (j + 1) * B] = jnp.concatenate(
                        [jnp.where(mine, hi, 0.0), jnp.where(mine, lo, 0.0)], axis=0
                    ).astype(bf16)

        def step(h, carry):
            blocks = [order(h * STEP + n) for n in range(STEP)]
            for n, g in enumerate(blocks):
                ready(h * STEP + n, g)
            for n, g in enumerate(blocks):
                fill(g, n)
            total = acc[0:depth, :]
            for n, g in enumerate(blocks):
                total = total + lax.dot_general(
                    st[n, 0:depth, :], hot[g], (((1,), (1,)), ((), ())),
                    preferred_element_type=f32,
                )
            acc[0:depth, :] = total
            return carry

        lax.fori_loop(0, COLS // STEP, step, 0)

    def keep_backward(part, with_degree):
        for v in range(ROWS):
            part[v, 0:FEAT, :] = acc[v * 64 : v * 64 + 32, :] + acc[v * 64 + 32 : v * 64 + 64, :]
            if with_degree:
                part[v, FEAT:PART, :] = jnp.broadcast_to(
                    acc[512 + v : 513 + v, :] + acc[520 + v : 521 + v, :], (8, B)
                )

    def give_back(part, got, send, recv):
        def step(k, carry):
            @pl.when(jnp.logical_not(jnp.logical_and(same, k == q)))
            def _():
                to_homes(k, part.at[k], got, send, recv).start()

            return carry

        lax.fori_loop(0, ROWS, step, 0)

        @pl.when(same)
        def _():
            got[r] = part[q]

    def add_forward(part, got, send, recv):
        def step(n, total):
            k = (c + 2 * n) % COLS
            arrival(got, k, send, recv).wait_recv()
            return total + got[k]

        return lax.fori_loop(1, ROWS, step, part[c])

    def add_backward(got, send, recv):
        def step(k, total):
            @pl.when(jnp.logical_not(jnp.logical_and(same, k == r)))
            def _():
                arrival(got, k, send, recv).wait_recv()

            return total + got[k]

        return lax.fori_loop(0, ROWS, step, jnp.zeros(got.shape[1:], f32))

    def signal_ready(t, g):
        @pl.when(t % 2 == 1)
        def _():
            row_arrival(rows, g, S, rs_send, rs_recv).wait_recv()

    own_signal = lambda g: rows[g, 2 * EMB : ALL, :]
    backward(own_signal, signal_ready, True)
    keep_backward(b_part, True)
    give_back(b_part, b_got, b_send, b_recv)

    own = rows[c, 2 * EMB : ALL, :]
    summed = add_forward(f_part, f_got, f_send, f_recv)
    f_scale = GO / (1.0 + summed[FEAT : FEAT + 1])
    f_home[...] = KEEP * own + (summed[:FEAT] + own) * f_scale
    share_with_users(f_home, colx, c2_send, c2_recv)

    summed = add_backward(b_got, b_send, b_recv)
    b_scale = GO / (1.0 + summed[FEAT : FEAT + 1])
    rowx[c] = KEEP * own + (summed[:FEAT] + own) * b_scale
    A = pl.ds(0, FEAT)

    def to_chip(n):
        return pass_on((c + 2 * n) % COLS, rowx, c, rowx, A, n, r2_send, r2_recv)

    def on_to_twin(n):
        return pass_on(twin(c), rowx, (c + 2 * n) % COLS, rowx, A, ROWS + n, r2_send, r2_recv)

    for n in range(1, ROWS):
        to_chip(n).start()
    on_to_twin(0).start()

    homes_arrived(colx, pl.ds(0, FEAT), c2_send, c2_recv, lambda k: k == q)
    for v in range(ROWS):
        put_columns(colx[v], v)

    forward_hop(f_part2, f_pair2, f_got2, p2_send, p2_recv, f2_send, f2_recv, lambda h: None)

    for n in range(1, ROWS):
        row_arrival(rowx, (c + 2 * n) % COLS, A, r2_send, r2_recv).wait_recv()
        on_to_twin(n).start()

    def ready(t, g):
        @pl.when(t % 2 == 1)
        def _():
            row_arrival(rowx, g, A, r2_send, r2_recv).wait_recv()

    backward(lambda g: rowx[g], ready, False)
    keep_backward(b_part2, False)
    give_back(b_part2, b_got2, b2_send, b2_recv)

    fetches[6].wait()
    fetches[7].wait()
    first = f_home[...]
    summed = add_forward(f_part2, f_got2, f2_send, f2_recv)
    second = KEEP * own + (summed + first) * f_scale
    mixed = full_dot(wf[...], jnp.concatenate([own, first, second], axis=0))
    first = rowx[c]
    summed = add_backward(b_got2, b2_send, b2_recv)
    second = KEEP * own + (summed + first) * b_scale
    out[...] = mixed + full_dot(wb[...], jnp.concatenate([own, first, second], axis=0))

    users_each(lambda k: to_users(k, f_home, colx, c2_send, c2_recv).wait_send())

    def sent(i, slot):
        home_to(i, slot, M, cm_send, cm_recv).wait_send()
        home_to(i, slot, S, cs_send, cs_recv).wait_send()

    homes_each(c, sent)
    homes_each(partner, sent)

    def sent_to_homes(k, carry):
        @pl.when(jnp.logical_not(jnp.logical_and(same, k == q)))
        def _():
            to_homes(k, b_part.at[k], b_got, b_send, b_recv).wait_send()
            to_homes(k, b_part2.at[k], b_got2, b2_send, b2_recv).wait_send()

        return carry

    def sent_to_row(n, carry):
        k = (c + 2 * n) % COLS
        to_row(k, f_part.at[k], f_got, f_send, f_recv).wait_send()
        to_row(k, f_part2.at[k], f_got2, f2_send, f2_recv).wait_send()
        to_chip(n).wait_send()
        return carry

    def sent_to_pair(n, carry):
        k = (twin(c) + 2 * n) % COLS
        pair_sum(k, f_part, f_pair, p_send, p_recv).wait_send()
        pair_sum(k, f_part2, f_pair2, p2_send, p2_recv).wait_send()
        on_to_twin(n).wait_send()
        return carry

    lax.fori_loop(0, ROWS, sent_to_pair, 0)
    lax.fori_loop(0, ROWS, sent_to_homes, 0)
    lax.fori_loop(1, ROWS, sent_to_row, 0)
    for copy in m_mine + m_relayed + s_mine + s_relayed:
        copy.wait_send()

    def sent_to_twin(i, carry):
        to_twin(i, rows, M, rm_send, rm_recv).wait_send()
        to_twin(i, rows, S, rs_send, rs_recv).wait_send()
        return carry

    lax.fori_loop(2, ROWS, sent_to_twin, 0)


def per_device(*args):
    vmem = pltpu.VMEM
    keep_count = args[5].shape[0]
    dma = pltpu.SemaphoreType.DMA
    scratch = [
        vmem((EMB, B), f32), vmem((EMB, B), f32), vmem((EMB, EMB), f32), vmem((EMB, EMB), f32),
        vmem((keep_count, COLS * B), i32), vmem((FEAT, 3 * FEAT), f32), vmem((FEAT, 3 * FEAT), f32),
        vmem((COLS, ALL, B), f32),
        vmem((ROWS, ALL, B), f32),
        vmem((ROWS * B, 6 * EMB), bf16),
        vmem((6 * EMB, B), bf16),
        vmem((512, B), bf16),
        vmem((STEP, 528, SLOTS * B), bf16),
        vmem((COLS, B, SLOTS * B), bf16),
        vmem((COLS, 8, B), i32),
        vmem((COLS, 8, B), f32),
        vmem((528, B), f32),
        vmem((COLS, PART, B), f32), vmem((COLS, PART, B), f32),
        vmem((COLS, PART, B), f32),
        vmem((ROWS, PART, B), f32), vmem((ROWS, PART, B), f32),
        vmem((FEAT, B), f32),
        vmem((ROWS, FEAT, B), f32), vmem((COLS, FEAT, B), f32),
        vmem((COLS, FEAT, B), f32), vmem((COLS, FEAT, B), f32),
        vmem((COLS, FEAT, B), f32),
        vmem((ROWS, FEAT, B), f32), vmem((ROWS, FEAT, B), f32),
        dma((8,)),
    ]
    for count in (ROWS, ROWS, COLS, COLS, COLS, ROWS, ROWS, COLS, COLS, ROWS, COLS, COLS):
        scratch += [dma((count,)), dma((count,))]
    return pl.pallas_call(
        kernel,
        out_shape=jax.ShapeDtypeStruct((FEAT, B), f32),
        in_specs=[pl.BlockSpec(memory_space=pl.ANY)] * 8,
        out_specs=pl.BlockSpec(memory_space=pltpu.VMEM),
        scratch_shapes=scratch,
        compiler_params=pltpu.CompilerParams(
            collective_id=0, has_side_effects=True, vmem_limit_bytes=VMEM_BYTES
        ),
        name="graph_layer",
    )(*args[:6], args[6].T, args[7].T)


def solution(mesh):
    placed = (
        P(None, ("row", "col")),
        P(None, ("row", "col")),
        P(None, ("row", "col")),
        P(),
        P(),
        P(None, "row"),
        P(),
        P(),
    )
    return jax.shard_map(
        per_device, mesh=mesh, in_specs=placed, out_specs=P(None, ("row", "col")), check_vma=False
    )
```

```python
import jax
import jax.numpy as jnp
from jax import lax
from jax.experimental import pallas as pl
from jax.experimental.pallas import tpu as pltpu
from jax.sharding import PartitionSpec as P

KEEP = 0.05
GO = 1.0 - KEEP
HIGHEST = lax.Precision.HIGHEST
MESH = pl.DeviceIdType.MESH
f32, bf16, i32 = jnp.float32, jnp.bfloat16, jnp.int32

ROWS = 8
COLS = 16
B = 256
SLOTS = 3
EMB = 40
FEAT = 32
ALL = 2 * EMB + FEAT
VMEM_BYTES = 60 * 1024 * 1024
STEP = 4
PART = FEAT + 8


def halves(x):
    hi = x.astype(bf16).astype(f32)
    return hi, x - hi


def transposed_dot(a, b):
    return lax.dot_general(
        a, b, (((0,), (0,)), ((), ())), precision=HIGHEST, preferred_element_type=f32
    )


def full_dot(a, b):
    return jnp.dot(a, b, precision=HIGHEST, preferred_element_type=f32)


def kernel(
    emb_first, emb_second, signal, theta_first, theta_second, neighbors, w_forward, w_backward,
    out,
    emb1, emb2, theta1, theta2, near, wf, wb,
    rows, cols, right, left, xs, st, hot, idx, weight, acc,
    f_part, f_pair, f_got, b_part, b_got, f_home, colx, rowx, f_part2, f_pair2, f_got2, b_part2, b_got2,
    in_sem, cm_send, cm_recv, cs_send, cs_recv, rm_send, rm_recv, rs_send, rs_recv,
    f_send, f_recv, b_send, b_recv, c2_send, c2_recv, r2_send, r2_recv,
    f2_send, f2_recv, b2_send, b2_recv, p_send, p_recv, p2_send, p2_recv,
):
    r = lax.axis_index("row")
    c = lax.axis_index("col")
    half = c // ROWS
    q = c % ROWS
    base = c - q
    z, x_lo = r // 2, r % 2
    maker = (z + 2 * (c % 2) + (c // 2) % 2) % 4 * 2 + (x_lo + (c // 4) % 2) % 2
    block_start = (2 * maker + half) * (ROWS * B)
    same = q == 0

    def user(k):
        away = (z + 4 - k // 2) % 4
        return base + 4 * ((x_lo + k) % 2) + 2 * (away % 2) + away // 2

    others = jnp.where(same, 0, 1).astype(i32)

    barrier = pltpu.get_barrier_semaphore()

    def greet(i, carry):
        pl.semaphore_signal(barrier, inc=1, device_id=(r, (c + i) % COLS), device_id_type=MESH)
        return carry

    def greet_columns(k, carry):
        @pl.when(jnp.logical_not(jnp.logical_and(same, k == r)))
        def _():
            pl.semaphore_signal(barrier, inc=1, device_id=(k, user(k)), device_id_type=MESH)

        @pl.when(jnp.logical_not(jnp.logical_and(same, k == q)))
        def _():
            pl.semaphore_signal(barrier, inc=1, device_id=(maker, base + k), device_id_type=MESH)

        return carry

    lax.fori_loop(1, COLS, greet, 0)
    lax.fori_loop(0, ROWS, greet_columns, 0)

    fetches = [
        pltpu.make_async_copy(src, dst, in_sem.at[n])
        for n, (src, dst) in enumerate(
            [
                (emb_first, emb1), (emb_second, emb2), (theta_first, theta1),
                (theta_second, theta2), (signal, rows.at[c, pl.ds(2 * EMB, FEAT)]),
                (neighbors, near), (w_forward, wf), (w_backward, wb),
            ]
        )
    ]
    for fetch in fetches:
        fetch.start()
    for fetch in fetches[:5]:
        fetch.wait()
    rows[c, 0:EMB, :] = jnp.tanh(3.0 * transposed_dot(theta1[...], emb1[...]))
    rows[c, EMB : 2 * EMB, :] = jnp.tanh(3.0 * transposed_dot(theta2[...], emb2[...]))

    pl.semaphore_wait(barrier, COLS - 1 + 2 * (ROWS - 1) + 2 * others)

    def to_users(k, src, dst, send, recv):
        return pltpu.make_async_remote_copy(
            src_ref=src, dst_ref=dst.at[q], send_sem=send.at[k], recv_sem=recv.at[q],
            device_id=(k, user(k)), device_id_type=MESH,
        )

    def to_row(k, src, dst, send, recv):
        return pltpu.make_async_remote_copy(
            src_ref=src, dst_ref=dst.at[c], send_sem=send.at[k], recv_sem=recv.at[c],
            device_id=(r, k), device_id_type=MESH,
        )

    def to_homes(k, src, dst, send, recv):
        return pltpu.make_async_remote_copy(
            src_ref=src, dst_ref=dst.at[r], send_sem=send.at[k], recv_sem=recv.at[r],
            device_id=(maker, base + k), device_id_type=MESH,
        )

    def arrival(dst, slot, send, recv):
        return pltpu.make_async_remote_copy(
            src_ref=dst.at[slot], dst_ref=dst.at[slot], send_sem=send.at[slot],
            recv_sem=recv.at[slot], device_id=(r, (c + 1) % COLS), device_id_type=MESH,
        )

    def twin(k):
        return k + 1 - 2 * (k % 2)

    def across(k):
        return k + 2 - 4 * ((k // 2) % 2)

    def around(k, n):
        return (k + 4 * n) % COLS

    def order(t):
        i = t // 2
        k = i // 2
        slot = around(c, k + (k // 2) * (1 - 2 * (k % 2)))
        slot = slot + (i % 2) * (2 - 4 * ((slot // 2) % 2))
        return slot + (t % 2) * (1 - 2 * (slot % 2))

    def own_core_first(step):
        return 2 * (step % ROWS) + step // ROWS

    M = pl.ds(0, 2 * EMB)
    S = pl.ds(2 * EMB, FEAT)

    def pass_on(to, src_buf, slot, dst_buf, part, n, send, recv):
        return pltpu.make_async_remote_copy(
            src_ref=src_buf.at[slot, part], dst_ref=dst_buf.at[slot, part],
            send_sem=send.at[n], recv_sem=recv.at[slot],
            device_id=(r, to), device_id_type=MESH,
        )

    def row_arrival(buf, slot, part, send, recv):
        return pltpu.make_async_remote_copy(
            src_ref=buf.at[slot, part], dst_ref=buf.at[slot, part], send_sem=send.at[0],
            recv_sem=recv.at[slot], device_id=(r, twin(c)), device_id_type=MESH,
        )

    def users_each(do):
        def step(i, carry):
            k = (r + i) % ROWS

            @pl.when(jnp.logical_not(jnp.logical_and(same, k == r)))
            def _():
                do(k)

            return carry

        lax.fori_loop(0, ROWS, step, 0)

    y_low = (c // 4) % 2
    partner = c + 4 - 8 * y_low
    near_row = (x_lo + y_low) % 2

    def home_to(i, slot, part, send, recv):
        k = 2 * i + near_row
        n = i + 4 * (jnp.where(slot == c, 0, 1).astype(i32))
        return pltpu.make_async_remote_copy(
            src_ref=rows.at[slot, part], dst_ref=cols.at[slot % ROWS, part], send_sem=send.at[n],
            recv_sem=recv.at[slot % ROWS], device_id=(k, user(k)), device_id_type=MESH,
        )

    def homes_each(slot, do):
        def step(j, carry):
            i = (z + j) % 4

            @pl.when(jnp.logical_not(own_user(i)))
            def _():
                do(i, slot)

            return carry

        lax.fori_loop(0, 4, step, 0)

    def own_user(i):
        k = 2 * i + near_row
        return jnp.logical_and(k == r, user(k) == c)

    def homes_arrived(buf, part, send, recv, kept):
        def step(k, carry):
            @pl.when(jnp.logical_not(jnp.logical_and(same, kept(k))))
            def _():
                pltpu.make_async_remote_copy(
                    src_ref=buf.at[k, part], dst_ref=buf.at[k, part], send_sem=send.at[k],
                    recv_sem=recv.at[k], device_id=(r, twin(c)), device_id_type=MESH,
                ).wait_recv()

            return carry

        lax.fori_loop(0, ROWS, step, 0)

    def share_with_users(src, dst, send, recv):
        users_each(lambda k: to_users(k, src, dst, send, recv).start())

        @pl.when(same)
        def _():
            dst[q] = src[...]

    def row_copies(buf, part, send, recv):
        far = [around(c, 1), around(c, 3), around(c, 2)]
        make = lambda to, slot, n: pass_on(to, buf, slot, buf, part, n, send, recv)
        mine = [make(across(c), c, 0)] + [make(to, c, 1 + n) for n, to in enumerate(far)]
        mine += [make(twin(c), c, 4)]
        relayed = [make(to, across(c), 5 + n) for n, to in enumerate(far)]
        relayed += [make(twin(c), across(c), 8)]
        return mine, relayed

    def to_twin(i, buf, part, send, recv):
        return pass_on(twin(c), buf, order(2 * i), buf, part, 7 + i, send, recv)

    m_mine, m_relayed = row_copies(rows, M, rm_send, rm_recv)
    s_mine, s_relayed = row_copies(rows, S, rs_send, rs_recv)
    for copy in (m_mine[1], m_mine[2], m_mine[0]):
        copy.start()
    homes_each(c, lambda i, slot: home_to(i, slot, M, cm_send, cm_recv).start())
    for copy in m_mine[3:]:
        copy.start()

    @pl.when(same)
    def _():
        cols[q] = rows[c]

    def partner_block(part, buf_send, buf_recv, send, recv):
        row_arrival(rows, partner, part, buf_send, buf_recv).wait_recv()
        homes_each(partner, lambda i, slot: home_to(i, slot, part, send, recv).start())

        @pl.when(same)
        def _():
            cols[partner % ROWS, part] = rows[partner, part]

    partner_block(M, rm_send, rm_recv, cm_send, cm_recv)
    row_arrival(rows, across(c), M, rm_send, rm_recv).wait_recv()
    for copy in m_relayed:
        copy.start()
    for copy in s_mine:
        copy.start()
    homes_each(c, lambda i, slot: home_to(i, slot, S, cs_send, cs_recv).start())

    fetches[5].wait()

    def find(g, carry):
        span = pl.ds(pl.multiple_of(g * B, B), B)
        local = near[:, span] - block_start
        slot = [jnp.full((1, B), -1, i32) for _ in range(SLOTS)]
        for k in range(near.shape[0]):
            entry = local[k : k + 1]
            inside = jnp.logical_and(entry >= 0, entry < ROWS * B)
            slot = [
                jnp.where(inside, entry, slot[0]),
                jnp.where(inside, slot[0], slot[1]),
                jnp.where(inside, slot[1], slot[2]),
            ]
        place = lax.broadcasted_iota(i32, (B, B), 0)
        for j in range(SLOTS):
            hot[g, :, j * B : (j + 1) * B] = (place == (slot[j] & (B - 1))).astype(f32).astype(bf16)
        idx[g] = jnp.concatenate(slot + [jnp.full((8 - SLOTS, B), -1, i32)], axis=0)
        return carry

    lax.fori_loop(0, COLS, find, 0)

    def put_columns(values, v):
        hi, lo = halves(values)
        xs[v * 64 : v * 64 + 64, :] = jnp.concatenate([hi, lo], axis=0).astype(bf16)

    homes_arrived(cols, M, cm_send, cm_recv, lambda k: k % 4 == 0)
    for v in range(ROWS):
        turned = jnp.concatenate([cols[v, EMB : 2 * EMB, :], -cols[v, 0:EMB, :]], axis=0)
        hi, lo = halves(turned)
        right[v * B : (v + 1) * B, :] = jnp.concatenate([hi, hi, lo], axis=0).T.astype(bf16)

    def forward(g):
        picked = jnp.dot(xs[...], hot[g], preferred_element_type=f32)
        total = jnp.zeros((FEAT, B), f32)
        for j in range(SLOTS):
            window = idx[g, j : j + 1, :] >> 8
            part = jnp.zeros((2 * FEAT, B), f32)
            for v in range(ROWS):
                part = jnp.where(
                    window == v, picked[v * 64 : v * 64 + 64, j * B : (j + 1) * B], part
                )
            total = total + weight[g, j : j + 1, :] * (part[:FEAT] + part[FEAT:])
        return total

    def score_step(step, carry):
        t = own_core_first(step)
        g = order(t)

        @pl.when(jnp.logical_or(t % 2 == 1, jnp.logical_and(t >= 4, g != partner)))
        def _():
            row_arrival(rows, g, M, rm_send, rm_recv).wait_recv()

        @pl.when(jnp.logical_and(t % 2 == 0, t >= 4))
        def _():
            to_twin(t // 2, rows, M, rm_send, rm_recv).start()

        @pl.when(t == 4)
        def _():
            partner_block(S, rs_send, rs_recv, cs_send, cs_recv)
            row_arrival(rows, across(c), S, rs_send, rs_recv).wait_recv()
            for copy in s_relayed:
                copy.start()

        hi, lo = halves(rows[g, 0 : 2 * EMB, :])
        left[...] = jnp.concatenate([hi, lo, hi], axis=0).astype(bf16)
        eight = lax.broadcasted_iota(i32, (8, B), 0)
        gap = [idx[g, j : j + 1, :] - eight for j in range(SLOTS)]
        found = [jnp.zeros((8, B), f32) for _ in range(SLOTS)]
        for v in range(ROWS):
            score = jnp.dot(
                right[v * B : (v + 1) * B, :], left[...], preferred_element_type=f32
            )
            for t in range(B // 8):
                for j in range(SLOTS):
                    found[j] = jnp.where(
                        gap[j] == v * B + 8 * t, score[8 * t : 8 * t + 8], found[j]
                    )
        sums = jnp.zeros((1, B), f32)
        for j in range(SLOTS):
            value = jnp.tanh(3.0 * jnp.sum(found[j], axis=0, keepdims=True))
            value = jnp.where(idx[g, j : j + 1, :] >= 0, jnp.maximum(value, 0.0), 0.0)
            weight[g, j : j + 1, :] = value
            sums = sums + value
        f_part[g, FEAT:PART, :] = jnp.broadcast_to(sums, (8, B))
        return carry

    lax.fori_loop(0, COLS, score_step, 0)
    homes_arrived(cols, S, cs_send, cs_recv, lambda k: k % 4 == 0)
    for v in range(ROWS):
        put_columns(cols[v, 2 * EMB : ALL, :], v)

    def pair_sum(g, part, pair, send, recv):
        return pltpu.make_async_remote_copy(
            src_ref=part.at[g], dst_ref=pair.at[g], send_sem=send.at[g], recv_sem=recv.at[g],
            device_id=(r, twin(c)), device_id_type=MESH,
        )

    def forward_hop(part, pair, got, p_send, p_recv, send, recv, before):
        def for_twin(h, carry):
            before(h)
            blocks = [order(2 * (h * STEP + n) + 1) for n in range(STEP)]
            sums = [forward(g) for g in blocks]
            for g, total in zip(blocks, sums):
                part[g, 0:FEAT, :] = total
            for g in blocks:
                pair_sum(g, part, pair, p_send, p_recv).start()
            return carry

        def for_others(h, carry):
            before(h + ROWS // STEP)
            late = [(h * STEP + n + 1) % ROWS for n in range(STEP)]
            blocks = [order(2 * i) for i in late]
            sums = [forward(g) for g in blocks]
            for g, total in zip(blocks, sums):
                part[g, 0:FEAT, :] = total
            for g, i in zip(blocks, late):
                pair_sum(g, part, pair, p_send, p_recv).wait_recv()
                part[g] = part[g] + pair[g]

                @pl.when(i > 0)
                def _():
                    to_row(g, part.at[g], got, send, recv).start()

            return carry

        lax.fori_loop(0, ROWS // STEP, for_twin, 0)
        lax.fori_loop(0, ROWS // STEP, for_others, 0)

    def signals_on(h):
        for n in range(0, STEP, 2):
            t = h * STEP + n

            @pl.when(t >= 4)
            def _():
                @pl.when(order(t) != partner)
                def _():
                    row_arrival(rows, order(t), S, rs_send, rs_recv).wait_recv()

                to_twin(t // 2, rows, S, rs_send, rs_recv).start()

    forward_hop(f_part, f_pair, f_got, p_send, p_recv, f_send, f_recv, signals_on)

    def backward(rows_of, ready, with_degree):
        acc[...] = jnp.zeros_like(acc)
        depth = 528 if with_degree else 512

        def fill(g, n):
            x = rows_of(g)
            for j in range(SLOTS):
                window = idx[g, j : j + 1, :] >> 8
                value = weight[g, j : j + 1, :]
                hi, lo = halves(x * value)
                both = jnp.concatenate([hi, lo], axis=0)
                for v in range(ROWS):
                    st[n, v * 64 : v * 64 + 64, j * B : (j + 1) * B] = jnp.where(
                        window == v, both, 0.0
                    ).astype(bf16)
                if with_degree:
                    hi, lo = halves(value)
                    mine = lax.broadcasted_iota(i32, (8, B), 0) == window
                    st[n, 512:528, j * B : (j + 1) * B] = jnp.concatenate(
                        [jnp.where(mine, hi, 0.0), jnp.where(mine, lo, 0.0)], axis=0
                    ).astype(bf16)

        def step(h, carry):
            times = [own_core_first(h * STEP + n) for n in range(STEP)]
            blocks = [order(t) for t in times]
            for t, g in zip(times, blocks):
                ready(t, g)
            for n, g in enumerate(blocks):
                fill(g, n)
            total = acc[0:depth, :]
            for n, g in enumerate(blocks):
                total = total + lax.dot_general(
                    st[n, 0:depth, :], hot[g], (((1,), (1,)), ((), ())),
                    preferred_element_type=f32,
                )
            acc[0:depth, :] = total
            return carry

        lax.fori_loop(0, COLS // STEP, step, 0)

    def keep_backward(part, with_degree):
        for v in range(ROWS):
            part[v, 0:FEAT, :] = acc[v * 64 : v * 64 + 32, :] + acc[v * 64 + 32 : v * 64 + 64, :]
            if with_degree:
                part[v, FEAT:PART, :] = jnp.broadcast_to(
                    acc[512 + v : 513 + v, :] + acc[520 + v : 521 + v, :], (8, B)
                )

    def give_back(part, got, send, recv):
        def step(k, carry):
            @pl.when(jnp.logical_not(jnp.logical_and(same, k == q)))
            def _():
                to_homes(k, part.at[k], got, send, recv).start()

            return carry

        lax.fori_loop(0, ROWS, step, 0)

        @pl.when(same)
        def _():
            got[r] = part[q]

    def add_forward(part, got, send, recv):
        def step(n, total):
            k = (c + 2 * n) % COLS
            arrival(got, k, send, recv).wait_recv()
            return total + got[k]

        return lax.fori_loop(1, ROWS, step, part[c])

    def add_backward(got, send, recv):
        def step(k, total):
            @pl.when(jnp.logical_not(jnp.logical_and(same, k == r)))
            def _():
                arrival(got, k, send, recv).wait_recv()

            return total + got[k]

        return lax.fori_loop(0, ROWS, step, jnp.zeros(got.shape[1:], f32))

    def signal_ready(t, g):
        @pl.when(t % 2 == 1)
        def _():
            row_arrival(rows, g, S, rs_send, rs_recv).wait_recv()

    own_signal = lambda g: rows[g, 2 * EMB : ALL, :]
    backward(own_signal, signal_ready, True)
    keep_backward(b_part, True)
    give_back(b_part, b_got, b_send, b_recv)

    own = rows[c, 2 * EMB : ALL, :]
    summed = add_forward(f_part, f_got, f_send, f_recv)
    f_scale = GO / (1.0 + summed[FEAT : FEAT + 1])
    f_home[...] = KEEP * own + (summed[:FEAT] + own) * f_scale
    share_with_users(f_home, colx, c2_send, c2_recv)

    summed = add_backward(b_got, b_send, b_recv)
    b_scale = GO / (1.0 + summed[FEAT : FEAT + 1])
    rowx[c] = KEEP * own + (summed[:FEAT] + own) * b_scale
    A = pl.ds(0, FEAT)

    def to_chip(n):
        return pass_on((c + 2 * n) % COLS, rowx, c, rowx, A, n, r2_send, r2_recv)

    def on_to_twin(n):
        return pass_on(twin(c), rowx, (c + 2 * n) % COLS, rowx, A, ROWS + n, r2_send, r2_recv)

    for n in range(1, ROWS):
        to_chip(n).start()
    on_to_twin(0).start()

    homes_arrived(colx, pl.ds(0, FEAT), c2_send, c2_recv, lambda k: k == q)
    for v in range(ROWS):
        put_columns(colx[v], v)

    forward_hop(f_part2, f_pair2, f_got2, p2_send, p2_recv, f2_send, f2_recv, lambda h: None)

    for n in range(1, ROWS):
        row_arrival(rowx, (c + 2 * n) % COLS, A, r2_send, r2_recv).wait_recv()
        on_to_twin(n).start()

    def ready(t, g):
        @pl.when(t % 2 == 1)
        def _():
            row_arrival(rowx, g, A, r2_send, r2_recv).wait_recv()

    backward(lambda g: rowx[g], ready, False)
    keep_backward(b_part2, False)
    give_back(b_part2, b_got2, b2_send, b2_recv)

    fetches[6].wait()
    fetches[7].wait()
    first = f_home[...]
    summed = add_forward(f_part2, f_got2, f2_send, f2_recv)
    second = KEEP * own + (summed + first) * f_scale
    mixed = full_dot(wf[...], jnp.concatenate([own, first, second], axis=0))
    first = rowx[c]
    summed = add_backward(b_got2, b2_send, b2_recv)
    second = KEEP * own + (summed + first) * b_scale
    out[...] = mixed + full_dot(wb[...], jnp.concatenate([own, first, second], axis=0))

    users_each(lambda k: to_users(k, f_home, colx, c2_send, c2_recv).wait_send())

    def sent(i, slot):
        home_to(i, slot, M, cm_send, cm_recv).wait_send()
        home_to(i, slot, S, cs_send, cs_recv).wait_send()

    homes_each(c, sent)
    homes_each(partner, sent)

    def sent_to_homes(k, carry):
        @pl.when(jnp.logical_not(jnp.logical_and(same, k == q)))
        def _():
            to_homes(k, b_part.at[k], b_got, b_send, b_recv).wait_send()
            to_homes(k, b_part2.at[k], b_got2, b2_send, b2_recv).wait_send()

        return carry

    def sent_to_row(n, carry):
        k = (c + 2 * n) % COLS
        to_row(k, f_part.at[k], f_got, f_send, f_recv).wait_send()
        to_row(k, f_part2.at[k], f_got2, f2_send, f2_recv).wait_send()
        to_chip(n).wait_send()
        return carry

    def sent_to_pair(n, carry):
        k = (twin(c) + 2 * n) % COLS
        pair_sum(k, f_part, f_pair, p_send, p_recv).wait_send()
        pair_sum(k, f_part2, f_pair2, p2_send, p2_recv).wait_send()
        on_to_twin(n).wait_send()
        return carry

    lax.fori_loop(0, ROWS, sent_to_pair, 0)
    lax.fori_loop(0, ROWS, sent_to_homes, 0)
    lax.fori_loop(1, ROWS, sent_to_row, 0)
    for copy in m_mine + m_relayed + s_mine + s_relayed:
        copy.wait_send()

    def sent_to_twin(i, carry):
        to_twin(i, rows, M, rm_send, rm_recv).wait_send()
        to_twin(i, rows, S, rs_send, rs_recv).wait_send()
        return carry

    lax.fori_loop(2, ROWS, sent_to_twin, 0)


def per_device(*args):
    vmem = pltpu.VMEM
    keep_count = args[5].shape[0]
    dma = pltpu.SemaphoreType.DMA
    scratch = [
        vmem((EMB, B), f32), vmem((EMB, B), f32), vmem((EMB, EMB), f32), vmem((EMB, EMB), f32),
        vmem((keep_count, COLS * B), i32), vmem((FEAT, 3 * FEAT), f32), vmem((FEAT, 3 * FEAT), f32),
        vmem((COLS, ALL, B), f32),
        vmem((ROWS, ALL, B), f32),
        vmem((ROWS * B, 6 * EMB), bf16),
        vmem((6 * EMB, B), bf16),
        vmem((512, B), bf16),
        vmem((STEP, 528, SLOTS * B), bf16),
        vmem((COLS, B, SLOTS * B), bf16),
        vmem((COLS, 8, B), i32),
        vmem((COLS, 8, B), f32),
        vmem((528, B), f32),
        vmem((COLS, PART, B), f32), vmem((COLS, PART, B), f32),
        vmem((COLS, PART, B), f32),
        vmem((ROWS, PART, B), f32), vmem((ROWS, PART, B), f32),
        vmem((FEAT, B), f32),
        vmem((ROWS, FEAT, B), f32), vmem((COLS, FEAT, B), f32),
        vmem((COLS, FEAT, B), f32), vmem((COLS, FEAT, B), f32),
        vmem((COLS, FEAT, B), f32),
        vmem((ROWS, FEAT, B), f32), vmem((ROWS, FEAT, B), f32),
        dma((8,)),
    ]
    for count in (ROWS, ROWS, COLS, COLS, COLS, ROWS, ROWS, COLS, COLS, ROWS, COLS, COLS):
        scratch += [dma((count,)), dma((count,))]
    return pl.pallas_call(
        kernel,
        out_shape=jax.ShapeDtypeStruct((FEAT, B), f32),
        in_specs=[pl.BlockSpec(memory_space=pl.ANY)] * 8,
        out_specs=pl.BlockSpec(memory_space=pltpu.VMEM),
        scratch_shapes=scratch,
        compiler_params=pltpu.CompilerParams(
            collective_id=0, has_side_effects=True, vmem_limit_bytes=VMEM_BYTES
        ),
        name="graph_layer",
    )(*args[:6], args[6].T, args[7].T)


def solution(mesh):
    placed = (
        P(None, ("row", "col")),
        P(None, ("row", "col")),
        P(None, ("row", "col")),
        P(),
        P(),
        P(None, "row"),
        P(),
        P(),
    )
    return jax.shard_map(
        per_device, mesh=mesh, in_specs=placed, out_specs=P(None, ("row", "col")), check_vma=False
    )
```

```python
import jax
import jax.numpy as jnp
from jax import lax
from jax.experimental import pallas as pl
from jax.experimental.pallas import tpu as pltpu
from jax.sharding import PartitionSpec as P

KEEP = 0.05
GO = 1.0 - KEEP
HIGHEST = lax.Precision.HIGHEST
MESH = pl.DeviceIdType.MESH
f32, bf16, i32 = jnp.float32, jnp.bfloat16, jnp.int32

ROWS = 8
COLS = 16
B = 256
SLOTS = 3
EMB = 40
FEAT = 32
ALL = 2 * EMB + FEAT
VMEM_BYTES = 60 * 1024 * 1024
STEP = 4
PART = FEAT + 8


def halves(x):
    hi = x.astype(bf16).astype(f32)
    return hi, x - hi


def transposed_dot(a, b):
    return lax.dot_general(
        a, b, (((0,), (0,)), ((), ())), precision=HIGHEST, preferred_element_type=f32
    )


def full_dot(a, b):
    return jnp.dot(a, b, precision=HIGHEST, preferred_element_type=f32)


def kernel(
    emb_first, emb_second, signal, theta_first, theta_second, neighbors, w_forward, w_backward,
    out,
    emb1, emb2, theta1, theta2, near, wf, wb,
    rows, cols, right, left, xs, st, hot, idx, weight, acc,
    f_part, f_pair, f_got, b_part, b_got, f_home, colx, rowx, f_part2, f_pair2, f_got2, b_part2, b_got2,
    in_sem, cm_send, cm_recv, cs_send, cs_recv, rm_send, rm_recv, rs_send, rs_recv,
    f_send, f_recv, b_send, b_recv, c2_send, c2_recv, r2_send, r2_recv,
    f2_send, f2_recv, b2_send, b2_recv, p_send, p_recv, p2_send, p2_recv,
):
    r = lax.axis_index("row")
    c = lax.axis_index("col")
    half = c // ROWS
    q = c % ROWS
    base = c - q
    z, x_lo = r // 2, r % 2
    maker = (z + 2 * (c % 2) + (c // 2) % 2) % 4 * 2 + (x_lo + (c // 4) % 2) % 2
    block_start = (2 * maker + half) * (ROWS * B)
    same = q == 0

    def user(k):
        away = (z + 4 - k // 2) % 4
        return base + 4 * ((x_lo + k) % 2) + 2 * (away % 2) + away // 2

    others = jnp.where(same, 0, 1).astype(i32)

    barrier = pltpu.get_barrier_semaphore()

    def greet(i, carry):
        pl.semaphore_signal(barrier, inc=1, device_id=(r, (c + i) % COLS), device_id_type=MESH)
        return carry

    def greet_columns(k, carry):
        @pl.when(jnp.logical_not(jnp.logical_and(same, k == r)))
        def _():
            pl.semaphore_signal(barrier, inc=1, device_id=(k, user(k)), device_id_type=MESH)

        @pl.when(jnp.logical_not(jnp.logical_and(same, k == q)))
        def _():
            pl.semaphore_signal(barrier, inc=1, device_id=(maker, base + k), device_id_type=MESH)

        return carry

    lax.fori_loop(1, COLS, greet, 0)
    lax.fori_loop(0, ROWS, greet_columns, 0)

    fetches = [
        pltpu.make_async_copy(src, dst, in_sem.at[n])
        for n, (src, dst) in enumerate(
            [
                (emb_first, emb1), (emb_second, emb2), (theta_first, theta1),
                (theta_second, theta2), (signal, rows.at[c, pl.ds(2 * EMB, FEAT)]),
                (neighbors, near), (w_forward, wf), (w_backward, wb),
            ]
        )
    ]
    for fetch in fetches:
        fetch.start()
    for fetch in fetches[:5]:
        fetch.wait()
    rows[c, 0:EMB, :] = jnp.tanh(3.0 * transposed_dot(theta1[...], emb1[...]))
    rows[c, EMB : 2 * EMB, :] = jnp.tanh(3.0 * transposed_dot(theta2[...], emb2[...]))

    pl.semaphore_wait(barrier, COLS - 1 + 2 * (ROWS - 1) + 2 * others)

    def to_users(k, src, dst, send, recv):
        return pltpu.make_async_remote_copy(
            src_ref=src, dst_ref=dst.at[q], send_sem=send.at[k], recv_sem=recv.at[q],
            device_id=(k, user(k)), device_id_type=MESH,
        )

    def to_row(k, src, dst, send, recv):
        return pltpu.make_async_remote_copy(
            src_ref=src, dst_ref=dst.at[c], send_sem=send.at[k], recv_sem=recv.at[c],
            device_id=(r, k), device_id_type=MESH,
        )

    def to_homes(k, src, dst, send, recv):
        return pltpu.make_async_remote_copy(
            src_ref=src, dst_ref=dst.at[r], send_sem=send.at[k], recv_sem=recv.at[r],
            device_id=(maker, base + k), device_id_type=MESH,
        )

    def arrival(dst, slot, send, recv):
        return pltpu.make_async_remote_copy(
            src_ref=dst.at[slot], dst_ref=dst.at[slot], send_sem=send.at[slot],
            recv_sem=recv.at[slot], device_id=(r, (c + 1) % COLS), device_id_type=MESH,
        )

    def twin(k):
        return k + 1 - 2 * (k % 2)

    def across(k):
        return k + 2 - 4 * ((k // 2) % 2)

    def around(k, n):
        return (k + 4 * n) % COLS

    def order(t):
        i = t // 2
        k = i // 2
        slot = around(c, k + (k // 2) * (1 - 2 * (k % 2)))
        slot = slot + (i % 2) * (2 - 4 * ((slot // 2) % 2))
        return slot + (t % 2) * (1 - 2 * (slot % 2))

    def own_core_first(step):
        return 2 * (step % ROWS) + step // ROWS

    M = pl.ds(0, 2 * EMB)
    S = pl.ds(2 * EMB, FEAT)

    def pass_on(to, src_buf, slot, dst_buf, part, n, send, recv):
        return pltpu.make_async_remote_copy(
            src_ref=src_buf.at[slot, part], dst_ref=dst_buf.at[slot, part],
            send_sem=send.at[n], recv_sem=recv.at[slot],
            device_id=(r, to), device_id_type=MESH,
        )

    def row_arrival(buf, slot, part, send, recv):
        return pltpu.make_async_remote_copy(
            src_ref=buf.at[slot, part], dst_ref=buf.at[slot, part], send_sem=send.at[0],
            recv_sem=recv.at[slot], device_id=(r, twin(c)), device_id_type=MESH,
        )

    def users_each(do):
        def step(i, carry):
            k = (r + i) % ROWS

            @pl.when(jnp.logical_not(jnp.logical_and(same, k == r)))
            def _():
                do(k)

            return carry

        lax.fori_loop(0, ROWS, step, 0)

    y_low = (c // 4) % 2
    partner = c + 4 - 8 * y_low
    near_row = (x_lo + y_low) % 2

    def home_to(i, slot, part, send, recv):
        k = 2 * i + near_row
        n = i + 4 * (jnp.where(slot == c, 0, 1).astype(i32))
        return pltpu.make_async_remote_copy(
            src_ref=rows.at[slot, part], dst_ref=cols.at[slot % ROWS, part], send_sem=send.at[n],
            recv_sem=recv.at[slot % ROWS], device_id=(k, user(k)), device_id_type=MESH,
        )

    def homes_each(slot, do):
        def step(j, carry):
            i = (z + j) % 4

            @pl.when(jnp.logical_not(own_user(i)))
            def _():
                do(i, slot)

            return carry

        lax.fori_loop(0, 4, step, 0)

    def own_user(i):
        k = 2 * i + near_row
        return jnp.logical_and(k == r, user(k) == c)

    def homes_arrived(buf, part, send, recv, kept):
        def step(k, carry):
            @pl.when(jnp.logical_not(jnp.logical_and(same, kept(k))))
            def _():
                pltpu.make_async_remote_copy(
                    src_ref=buf.at[k, part], dst_ref=buf.at[k, part], send_sem=send.at[k],
                    recv_sem=recv.at[k], device_id=(r, twin(c)), device_id_type=MESH,
                ).wait_recv()

            return carry

        lax.fori_loop(0, ROWS, step, 0)

    def share_with_users(src, dst, send, recv):
        users_each(lambda k: to_users(k, src, dst, send, recv).start())

        @pl.when(same)
        def _():
            dst[q] = src[...]

    def row_copies(buf, part, send, recv):
        far = [around(c, 1), around(c, 3), around(c, 2)]
        make = lambda to, slot, n: pass_on(to, buf, slot, buf, part, n, send, recv)
        mine = [make(across(c), c, 0)] + [make(to, c, 1 + n) for n, to in enumerate(far)]
        mine += [make(twin(c), c, 4)]
        relayed = [make(to, across(c), 5 + n) for n, to in enumerate(far)]
        relayed += [make(twin(c), across(c), 8)]
        return mine, relayed

    def to_twin(i, buf, part, send, recv):
        return pass_on(twin(c), buf, order(2 * i), buf, part, 7 + i, send, recv)

    m_mine, m_relayed = row_copies(rows, M, rm_send, rm_recv)
    s_mine, s_relayed = row_copies(rows, S, rs_send, rs_recv)
    for copy in (m_mine[1], m_mine[2], m_mine[0]):
        copy.start()
    homes_each(c, lambda i, slot: home_to(i, slot, M, cm_send, cm_recv).start())
    for copy in m_mine[3:]:
        copy.start()

    @pl.when(same)
    def _():
        cols[q] = rows[c]

    def partner_block(part, buf_send, buf_recv, send, recv):
        row_arrival(rows, partner, part, buf_send, buf_recv).wait_recv()
        homes_each(partner, lambda i, slot: home_to(i, slot, part, send, recv).start())

        @pl.when(same)
        def _():
            cols[partner % ROWS, part] = rows[partner, part]

    partner_block(M, rm_send, rm_recv, cm_send, cm_recv)
    row_arrival(rows, across(c), M, rm_send, rm_recv).wait_recv()
    for copy in m_relayed:
        copy.start()
    for copy in s_mine:
        copy.start()
    homes_each(c, lambda i, slot: home_to(i, slot, S, cs_send, cs_recv).start())

    fetches[5].wait()

    def find(g, carry):
        span = pl.ds(pl.multiple_of(g * B, B), B)
        local = near[:, span] - block_start
        slot = [jnp.full((1, B), -1, i32) for _ in range(SLOTS)]
        for k in range(near.shape[0]):
            entry = local[k : k + 1]
            inside = jnp.logical_and(entry >= 0, entry < ROWS * B)
            slot = [
                jnp.where(inside, entry, slot[0]),
                jnp.where(inside, slot[0], slot[1]),
                jnp.where(inside, slot[1], slot[2]),
            ]
        place = lax.broadcasted_iota(i32, (B, B), 0)
        for j in range(SLOTS):
            hot[g, :, j * B : (j + 1) * B] = (place == (slot[j] & (B - 1))).astype(f32).astype(bf16)
        idx[g] = jnp.concatenate(slot + [jnp.full((8 - SLOTS, B), -1, i32)], axis=0)
        return carry

    lax.fori_loop(0, COLS, find, 0)

    def put_columns(values, v):
        hi, lo = halves(values)
        xs[v * 64 : v * 64 + 64, :] = jnp.concatenate([hi, lo], axis=0).astype(bf16)

    homes_arrived(cols, M, cm_send, cm_recv, lambda k: k % 4 == 0)
    for v in range(ROWS):
        turned = jnp.concatenate([cols[v, EMB : 2 * EMB, :], -cols[v, 0:EMB, :]], axis=0)
        hi, lo = halves(turned)
        right[v * B : (v + 1) * B, :] = jnp.concatenate([hi, hi, lo], axis=0).T.astype(bf16)

    def forward(g):
        picked = jnp.dot(xs[...], hot[g], preferred_element_type=f32)
        total = jnp.zeros((FEAT, B), f32)
        for j in range(SLOTS):
            window = idx[g, j : j + 1, :] >> 8
            part = jnp.zeros((2 * FEAT, B), f32)
            for v in range(ROWS):
                part = jnp.where(
                    window == v, picked[v * 64 : v * 64 + 64, j * B : (j + 1) * B], part
                )
            total = total + weight[g, j : j + 1, :] * (part[:FEAT] + part[FEAT:])
        return total

    def score_step(step, carry):
        t = own_core_first(step)
        g = order(t)

        @pl.when(jnp.logical_or(t % 2 == 1, jnp.logical_and(t >= 4, g != partner)))
        def _():
            row_arrival(rows, g, M, rm_send, rm_recv).wait_recv()

        @pl.when(jnp.logical_and(t % 2 == 0, t >= 4))
        def _():
            to_twin(t // 2, rows, M, rm_send, rm_recv).start()

        @pl.when(t == 4)
        def _():
            partner_block(S, rs_send, rs_recv, cs_send, cs_recv)
            row_arrival(rows, across(c), S, rs_send, rs_recv).wait_recv()
            for copy in s_relayed:
                copy.start()

        hi, lo = halves(rows[g, 0 : 2 * EMB, :])
        left[...] = jnp.concatenate([hi, lo, hi], axis=0).astype(bf16)
        eight = lax.broadcasted_iota(i32, (8, B), 0)
        gap = [idx[g, j : j + 1, :] - eight for j in range(SLOTS)]
        found = [jnp.zeros((8, B), f32) for _ in range(SLOTS)]
        for v in range(ROWS):
            score = jnp.dot(
                right[v * B : (v + 1) * B, :], left[...], preferred_element_type=f32
            )
            for t in range(B // 8):
                for j in range(SLOTS):
                    found[j] = jnp.where(
                        gap[j] == v * B + 8 * t, score[8 * t : 8 * t + 8], found[j]
                    )
        sums = jnp.zeros((1, B), f32)
        for j in range(SLOTS):
            value = jnp.tanh(3.0 * jnp.sum(found[j], axis=0, keepdims=True))
            value = jnp.where(idx[g, j : j + 1, :] >= 0, jnp.maximum(value, 0.0), 0.0)
            weight[g, j : j + 1, :] = value
            sums = sums + value
        f_part[g, FEAT:PART, :] = jnp.broadcast_to(sums, (8, B))
        return carry

    lax.fori_loop(0, COLS, score_step, 0)
    homes_arrived(cols, S, cs_send, cs_recv, lambda k: k % 4 == 0)
    for v in range(ROWS):
        put_columns(cols[v, 2 * EMB : ALL, :], v)

    def pair_sum(g, part, pair, send, recv):
        return pltpu.make_async_remote_copy(
            src_ref=part.at[g], dst_ref=pair.at[g], send_sem=send.at[g], recv_sem=recv.at[g],
            device_id=(r, twin(c)), device_id_type=MESH,
        )

    def forward_hop(part, pair, got, p_send, p_recv, send, recv, before):
        def for_twin(h, carry):
            before(h)
            blocks = [order(2 * (h * STEP + n) + 1) for n in range(STEP)]
            sums = [forward(g) for g in blocks]
            for g, total in zip(blocks, sums):
                part[g, 0:FEAT, :] = total
            for g in blocks:
                pair_sum(g, part, pair, p_send, p_recv).start()
            return carry

        def for_others(h, carry):
            before(h + ROWS // STEP)
            late = [(h * STEP + n + 1) % ROWS for n in range(STEP)]
            blocks = [order(2 * i) for i in late]
            sums = [forward(g) for g in blocks]
            for g, total in zip(blocks, sums):
                part[g, 0:FEAT, :] = total
            for g, i in zip(blocks, late):
                pair_sum(g, part, pair, p_send, p_recv).wait_recv()
                part[g] = part[g] + pair[g]

                @pl.when(i > 0)
                def _():
                    to_row(g, part.at[g], got, send, recv).start()

            return carry

        lax.fori_loop(0, ROWS // STEP, for_twin, 0)
        lax.fori_loop(0, ROWS // STEP, for_others, 0)

    def signals_on(h):
        for n in range(0, STEP, 2):
            t = h * STEP + n

            @pl.when(t >= 4)
            def _():
                @pl.when(order(t) != partner)
                def _():
                    row_arrival(rows, order(t), S, rs_send, rs_recv).wait_recv()

                to_twin(t // 2, rows, S, rs_send, rs_recv).start()

    forward_hop(f_part, f_pair, f_got, p_send, p_recv, f_send, f_recv, signals_on)

    def backward(rows_of, ready, with_degree):
        acc[...] = jnp.zeros_like(acc)
        depth = 528 if with_degree else 512

        def fill(g, n):
            x = rows_of(g)
            for j in range(SLOTS):
                window = idx[g, j : j + 1, :] >> 8
                value = weight[g, j : j + 1, :]
                hi, lo = halves(x * value)
                both = jnp.concatenate([hi, lo], axis=0)
                for v in range(ROWS):
                    st[n, v * 64 : v * 64 + 64, j * B : (j + 1) * B] = jnp.where(
                        window == v, both, 0.0
                    ).astype(bf16)
                if with_degree:
                    hi, lo = halves(value)
                    mine = lax.broadcasted_iota(i32, (8, B), 0) == window
                    st[n, 512:528, j * B : (j + 1) * B] = jnp.concatenate(
                        [jnp.where(mine, hi, 0.0), jnp.where(mine, lo, 0.0)], axis=0
                    ).astype(bf16)

        def step(h, carry):
            times = [own_core_first(h * STEP + n) for n in range(STEP)]
            blocks = [order(t) for t in times]
            for t, g in zip(times, blocks):
                ready(t, g)
            for n, g in enumerate(blocks):
                fill(g, n)
            total = acc[0:depth, :]
            for n, g in enumerate(blocks):
                total = total + lax.dot_general(
                    st[n, 0:depth, :], hot[g], (((1,), (1,)), ((), ())),
                    preferred_element_type=f32,
                )
            acc[0:depth, :] = total
            return carry

        lax.fori_loop(0, COLS // STEP, step, 0)

    def keep_backward(part, with_degree):
        for v in range(ROWS):
            part[v, 0:FEAT, :] = acc[v * 64 : v * 64 + 32, :] + acc[v * 64 + 32 : v * 64 + 64, :]
            if with_degree:
                part[v, FEAT:PART, :] = jnp.broadcast_to(
                    acc[512 + v : 513 + v, :] + acc[520 + v : 521 + v, :], (8, B)
                )

    def give_back(part, got, send, recv):
        def step(k, carry):
            @pl.when(jnp.logical_not(jnp.logical_and(same, k == q)))
            def _():
                to_homes(k, part.at[k], got, send, recv).start()

            return carry

        lax.fori_loop(0, ROWS, step, 0)

        @pl.when(same)
        def _():
            got[r] = part[q]

    def add_forward(part, got, send, recv):
        def step(n, total):
            k = (c + 2 * n) % COLS
            arrival(got, k, send, recv).wait_recv()
            return total + got[k]

        return lax.fori_loop(1, ROWS, step, part[c])

    def add_backward(got, send, recv):
        def step(k, total):
            @pl.when(jnp.logical_not(jnp.logical_and(same, k == r)))
            def _():
                arrival(got, k, send, recv).wait_recv()

            return total + got[k]

        return lax.fori_loop(0, ROWS, step, jnp.zeros(got.shape[1:], f32))

    def signal_ready(t, g):
        @pl.when(t % 2 == 1)
        def _():
            row_arrival(rows, g, S, rs_send, rs_recv).wait_recv()

    own_signal = lambda g: rows[g, 2 * EMB : ALL, :]
    backward(own_signal, signal_ready, True)
    keep_backward(b_part, True)
    give_back(b_part, b_got, b_send, b_recv)

    own = rows[c, 2 * EMB : ALL, :]
    summed = add_forward(f_part, f_got, f_send, f_recv)
    f_scale = GO / (1.0 + summed[FEAT : FEAT + 1])
    f_home[...] = KEEP * own + (summed[:FEAT] + own) * f_scale
    share_with_users(f_home, colx, c2_send, c2_recv)

    summed = add_backward(b_got, b_send, b_recv)
    b_scale = GO / (1.0 + summed[FEAT : FEAT + 1])
    rowx[c] = KEEP * own + (summed[:FEAT] + own) * b_scale
    A = pl.ds(0, FEAT)

    def to_chip(n):
        return pass_on((c + 2 * n) % COLS, rowx, c, rowx, A, n, r2_send, r2_recv)

    def on_to_twin(n):
        return pass_on(twin(c), rowx, (c + 2 * n) % COLS, rowx, A, ROWS + n, r2_send, r2_recv)

    for n in range(1, ROWS):
        to_chip(n).start()
    on_to_twin(0).start()

    homes_arrived(colx, pl.ds(0, FEAT), c2_send, c2_recv, lambda k: k == q)
    for v in range(ROWS):
        put_columns(colx[v], v)

    forward_hop(f_part2, f_pair2, f_got2, p2_send, p2_recv, f2_send, f2_recv, lambda h: None)

    for n in range(1, ROWS):
        row_arrival(rowx, (c + 2 * n) % COLS, A, r2_send, r2_recv).wait_recv()
        on_to_twin(n).start()

    def ready(t, g):
        @pl.when(t % 2 == 1)
        def _():
            row_arrival(rowx, g, A, r2_send, r2_recv).wait_recv()

    backward(lambda g: rowx[g], ready, False)
    keep_backward(b_part2, False)
    give_back(b_part2, b_got2, b2_send, b2_recv)

    users_each(lambda k: to_users(k, f_home, colx, c2_send, c2_recv).wait_send())

    def sent(i, slot):
        home_to(i, slot, M, cm_send, cm_recv).wait_send()
        home_to(i, slot, S, cs_send, cs_recv).wait_send()

    homes_each(c, sent)
    homes_each(partner, sent)

    def sent_to_homes(k, carry):
        @pl.when(jnp.logical_not(jnp.logical_and(same, k == q)))
        def _():
            to_homes(k, b_part.at[k], b_got, b_send, b_recv).wait_send()
            to_homes(k, b_part2.at[k], b_got2, b2_send, b2_recv).wait_send()

        return carry

    def sent_to_row(n, carry):
        k = (c + 2 * n) % COLS
        to_row(k, f_part.at[k], f_got, f_send, f_recv).wait_send()
        to_row(k, f_part2.at[k], f_got2, f2_send, f2_recv).wait_send()
        to_chip(n).wait_send()
        return carry

    def sent_to_pair(n, carry):
        k = (twin(c) + 2 * n) % COLS
        pair_sum(k, f_part, f_pair, p_send, p_recv).wait_send()
        pair_sum(k, f_part2, f_pair2, p2_send, p2_recv).wait_send()
        on_to_twin(n).wait_send()
        return carry

    lax.fori_loop(0, ROWS, sent_to_pair, 0)
    lax.fori_loop(0, ROWS, sent_to_homes, 0)
    lax.fori_loop(1, ROWS, sent_to_row, 0)
    for copy in m_mine + m_relayed + s_mine + s_relayed:
        copy.wait_send()

    def sent_to_twin(i, carry):
        to_twin(i, rows, M, rm_send, rm_recv).wait_send()
        to_twin(i, rows, S, rs_send, rs_recv).wait_send()
        return carry

    lax.fori_loop(2, ROWS, sent_to_twin, 0)

    fetches[6].wait()
    fetches[7].wait()
    first = f_home[...]
    summed = add_forward(f_part2, f_got2, f2_send, f2_recv)
    second = KEEP * own + (summed + first) * f_scale
    mixed = full_dot(wf[...], jnp.concatenate([own, first, second], axis=0))
    first = rowx[c]
    summed = add_backward(b_got2, b2_send, b2_recv)
    second = KEEP * own + (summed + first) * b_scale
    out[...] = mixed + full_dot(wb[...], jnp.concatenate([own, first, second], axis=0))


def per_device(*args):
    vmem = pltpu.VMEM
    keep_count = args[5].shape[0]
    dma = pltpu.SemaphoreType.DMA
    scratch = [
        vmem((EMB, B), f32), vmem((EMB, B), f32), vmem((EMB, EMB), f32), vmem((EMB, EMB), f32),
        vmem((keep_count, COLS * B), i32), vmem((FEAT, 3 * FEAT), f32), vmem((FEAT, 3 * FEAT), f32),
        vmem((COLS, ALL, B), f32),
        vmem((ROWS, ALL, B), f32),
        vmem((ROWS * B, 6 * EMB), bf16),
        vmem((6 * EMB, B), bf16),
        vmem((512, B), bf16),
        vmem((STEP, 528, SLOTS * B), bf16),
        vmem((COLS, B, SLOTS * B), bf16),
        vmem((COLS, 8, B), i32),
        vmem((COLS, 8, B), f32),
        vmem((528, B), f32),
        vmem((COLS, PART, B), f32), vmem((COLS, PART, B), f32),
        vmem((COLS, PART, B), f32),
        vmem((ROWS, PART, B), f32), vmem((ROWS, PART, B), f32),
        vmem((FEAT, B), f32),
        vmem((ROWS, FEAT, B), f32), vmem((COLS, FEAT, B), f32),
        vmem((COLS, FEAT, B), f32), vmem((COLS, FEAT, B), f32),
        vmem((COLS, FEAT, B), f32),
        vmem((ROWS, FEAT, B), f32), vmem((ROWS, FEAT, B), f32),
        dma((8,)),
    ]
    for count in (ROWS, ROWS, COLS, COLS, COLS, ROWS, ROWS, COLS, COLS, ROWS, COLS, COLS):
        scratch += [dma((count,)), dma((count,))]
    return pl.pallas_call(
        kernel,
        out_shape=jax.ShapeDtypeStruct((FEAT, B), f32),
        in_specs=[pl.BlockSpec(memory_space=pl.ANY)] * 8,
        out_specs=pl.BlockSpec(memory_space=pltpu.VMEM),
        scratch_shapes=scratch,
        compiler_params=pltpu.CompilerParams(
            collective_id=0, has_side_effects=True, vmem_limit_bytes=VMEM_BYTES
        ),
        name="graph_layer",
    )(*args[:6], args[6].T, args[7].T)


def solution(mesh):
    placed = (
        P(None, ("row", "col")),
        P(None, ("row", "col")),
        P(None, ("row", "col")),
        P(),
        P(),
        P(None, "row"),
        P(),
        P(),
    )
    return jax.shard_map(
        per_device, mesh=mesh, in_specs=placed, out_specs=P(None, ("row", "col")), check_vma=False
    )
```

```python
import jax
import jax.numpy as jnp
from jax import lax
from jax.experimental import pallas as pl
from jax.experimental.pallas import tpu as pltpu
from jax.sharding import PartitionSpec as P

KEEP = 0.05
GO = 1.0 - KEEP
HIGHEST = lax.Precision.HIGHEST
MESH = pl.DeviceIdType.MESH
f32, bf16, i32 = jnp.float32, jnp.bfloat16, jnp.int32

ROWS = 8
COLS = 16
B = 256
SLOTS = 3
EMB = 40
FEAT = 32
ALL = 2 * EMB + FEAT
VMEM_BYTES = 60 * 1024 * 1024
STEP = 4
PART = FEAT + 8


def halves(x):
    hi = x.astype(bf16).astype(f32)
    return hi, x - hi


def transposed_dot(a, b):
    return lax.dot_general(
        a, b, (((0,), (0,)), ((), ())), precision=HIGHEST, preferred_element_type=f32
    )


def full_dot(a, b):
    return jnp.dot(a, b, precision=HIGHEST, preferred_element_type=f32)


def kernel(
    emb_first, emb_second, signal, theta_first, theta_second, neighbors, w_forward, w_backward,
    out,
    emb1, emb2, theta1, theta2, near, wf, wb,
    rows, cols, right, left, xs, st, hot, idx, weight, acc,
    f_part, f_pair, f_got, b_part, b_got, f_home, colx, rowx, f_part2, f_pair2, f_got2, b_part2, b_got2,
    in_sem, cm_send, cm_recv, cs_send, cs_recv, rm_send, rm_recv, rs_send, rs_recv,
    f_send, f_recv, b_send, b_recv, c2_send, c2_recv, r2_send, r2_recv,
    f2_send, f2_recv, b2_send, b2_recv, p_send, p_recv, p2_send, p2_recv,
):
    r = lax.axis_index("row")
    c = lax.axis_index("col")
    half = c // ROWS
    q = c % ROWS
    base = c - q
    z, x_lo = r // 2, r % 2
    maker = (z + 2 * (c % 2) + (c // 2) % 2) % 4 * 2 + (x_lo + (c // 4) % 2) % 2
    block_start = (2 * maker + half) * (ROWS * B)
    same = q == 0

    def user(k):
        away = (z + 4 - k // 2) % 4
        return base + 4 * ((x_lo + k) % 2) + 2 * (away % 2) + away // 2

    others = jnp.where(same, 0, 1).astype(i32)

    barrier = pltpu.get_barrier_semaphore()

    def greet(i, carry):
        pl.semaphore_signal(barrier, inc=1, device_id=(r, (c + i) % COLS), device_id_type=MESH)
        return carry

    def greet_columns(k, carry):
        @pl.when(jnp.logical_not(jnp.logical_and(same, k == r)))
        def _():
            pl.semaphore_signal(barrier, inc=1, device_id=(k, user(k)), device_id_type=MESH)

        @pl.when(jnp.logical_not(jnp.logical_and(same, k == q)))
        def _():
            pl.semaphore_signal(barrier, inc=1, device_id=(maker, base + k), device_id_type=MESH)

        return carry

    lax.fori_loop(1, COLS, greet, 0)
    lax.fori_loop(0, ROWS, greet_columns, 0)

    fetches = [
        pltpu.make_async_copy(src, dst, in_sem.at[n])
        for n, (src, dst) in enumerate(
            [
                (emb_first, emb1), (emb_second, emb2), (theta_first, theta1),
                (theta_second, theta2), (signal, rows.at[c, pl.ds(2 * EMB, FEAT)]),
                (neighbors, near), (w_forward, wf), (w_backward, wb),
            ]
        )
    ]
    for fetch in fetches:
        fetch.start()
    for fetch in fetches[:5]:
        fetch.wait()
    rows[c, 0:EMB, :] = jnp.tanh(3.0 * transposed_dot(theta1[...], emb1[...]))
    rows[c, EMB : 2 * EMB, :] = jnp.tanh(3.0 * transposed_dot(theta2[...], emb2[...]))

    pl.semaphore_wait(barrier, COLS - 1 + 2 * (ROWS - 1) + 2 * others)

    def to_users(k, src, dst, send, recv):
        return pltpu.make_async_remote_copy(
            src_ref=src, dst_ref=dst.at[q], send_sem=send.at[k], recv_sem=recv.at[q],
            device_id=(k, user(k)), device_id_type=MESH,
        )

    def to_row(k, src, dst, send, recv):
        return pltpu.make_async_remote_copy(
            src_ref=src, dst_ref=dst.at[c], send_sem=send.at[k], recv_sem=recv.at[c],
            device_id=(r, k), device_id_type=MESH,
        )

    def to_homes(k, src, dst, send, recv):
        return pltpu.make_async_remote_copy(
            src_ref=src, dst_ref=dst.at[r], send_sem=send.at[k], recv_sem=recv.at[r],
            device_id=(maker, base + k), device_id_type=MESH,
        )

    def arrival(dst, slot, send, recv):
        return pltpu.make_async_remote_copy(
            src_ref=dst.at[slot], dst_ref=dst.at[slot], send_sem=send.at[slot],
            recv_sem=recv.at[slot], device_id=(r, (c + 1) % COLS), device_id_type=MESH,
        )

    def twin(k):
        return k + 1 - 2 * (k % 2)

    def across(k):
        return k + 2 - 4 * ((k // 2) % 2)

    def around(k, n):
        return (k + 4 * n) % COLS

    def order(t):
        i = t // 2
        k = i // 2
        slot = around(c, k + (k // 2) * (1 - 2 * (k % 2)))
        slot = slot + (i % 2) * (2 - 4 * ((slot // 2) % 2))
        return slot + (t % 2) * (1 - 2 * (slot % 2))

    def own_core_first(step):
        return 2 * (step % ROWS) + step // ROWS

    M = pl.ds(0, 2 * EMB)
    S = pl.ds(2 * EMB, FEAT)

    def pass_on(to, src_buf, slot, dst_buf, part, n, send, recv):
        return pltpu.make_async_remote_copy(
            src_ref=src_buf.at[slot, part], dst_ref=dst_buf.at[slot, part],
            send_sem=send.at[n], recv_sem=recv.at[slot],
            device_id=(r, to), device_id_type=MESH,
        )

    def row_arrival(buf, slot, part, send, recv):
        return pltpu.make_async_remote_copy(
            src_ref=buf.at[slot, part], dst_ref=buf.at[slot, part], send_sem=send.at[0],
            recv_sem=recv.at[slot], device_id=(r, twin(c)), device_id_type=MESH,
        )

    def users_each(do):
        def step(i, carry):
            k = (r + i) % ROWS

            @pl.when(jnp.logical_not(jnp.logical_and(same, k == r)))
            def _():
                do(k)

            return carry

        lax.fori_loop(0, ROWS, step, 0)

    y_low = (c // 4) % 2
    partner = c + 4 - 8 * y_low
    near_row = (x_lo + y_low) % 2

    def home_to(i, slot, part, send, recv):
        k = 2 * i + near_row
        n = i + 4 * (jnp.where(slot == c, 0, 1).astype(i32))
        return pltpu.make_async_remote_copy(
            src_ref=rows.at[slot, part], dst_ref=cols.at[slot % ROWS, part], send_sem=send.at[n],
            recv_sem=recv.at[slot % ROWS], device_id=(k, user(k)), device_id_type=MESH,
        )

    def homes_each(slot, do):
        def step(j, carry):
            i = (z + j) % 4

            @pl.when(jnp.logical_not(own_user(i)))
            def _():
                do(i, slot)

            return carry

        lax.fori_loop(0, 4, step, 0)

    def own_user(i):
        k = 2 * i + near_row
        return jnp.logical_and(k == r, user(k) == c)

    def homes_arrived(buf, part, send, recv, kept):
        def step(k, carry):
            @pl.when(jnp.logical_not(jnp.logical_and(same, kept(k))))
            def _():
                pltpu.make_async_remote_copy(
                    src_ref=buf.at[k, part], dst_ref=buf.at[k, part], send_sem=send.at[k],
                    recv_sem=recv.at[k], device_id=(r, twin(c)), device_id_type=MESH,
                ).wait_recv()

            return carry

        lax.fori_loop(0, ROWS, step, 0)

    def share_with_users(src, dst, send, recv):
        users_each(lambda k: to_users(k, src, dst, send, recv).start())

        @pl.when(same)
        def _():
            dst[q] = src[...]

    def row_copies(buf, part, send, recv):
        far = [around(c, 1), around(c, 3), around(c, 2)]
        make = lambda to, slot, n: pass_on(to, buf, slot, buf, part, n, send, recv)
        mine = [make(across(c), c, 0)] + [make(to, c, 1 + n) for n, to in enumerate(far)]
        mine += [make(twin(c), c, 4)]
        relayed = [make(to, across(c), 5 + n) for n, to in enumerate(far)]
        relayed += [make(twin(c), across(c), 8)]
        return mine, relayed

    def to_twin(i, buf, part, send, recv):
        return pass_on(twin(c), buf, order(2 * i), buf, part, 7 + i, send, recv)

    m_mine, m_relayed = row_copies(rows, M, rm_send, rm_recv)
    s_mine, s_relayed = row_copies(rows, S, rs_send, rs_recv)
    for copy in (m_mine[1], m_mine[2], m_mine[0]):
        copy.start()
    homes_each(c, lambda i, slot: home_to(i, slot, M, cm_send, cm_recv).start())
    for copy in m_mine[3:]:
        copy.start()

    @pl.when(same)
    def _():
        cols[q] = rows[c]

    def partner_block(part, buf_send, buf_recv, send, recv):
        row_arrival(rows, partner, part, buf_send, buf_recv).wait_recv()
        homes_each(partner, lambda i, slot: home_to(i, slot, part, send, recv).start())

        @pl.when(same)
        def _():
            cols[partner % ROWS, part] = rows[partner, part]

    partner_block(M, rm_send, rm_recv, cm_send, cm_recv)
    row_arrival(rows, across(c), M, rm_send, rm_recv).wait_recv()
    for copy in m_relayed:
        copy.start()
    for copy in s_mine:
        copy.start()
    homes_each(c, lambda i, slot: home_to(i, slot, S, cs_send, cs_recv).start())

    fetches[5].wait()

    def find(g, carry):
        span = pl.ds(pl.multiple_of(g * B, B), B)
        local = near[:, span] - block_start
        slot = [jnp.full((1, B), -1, i32) for _ in range(SLOTS)]
        for k in range(near.shape[0]):
            entry = local[k : k + 1]
            inside = jnp.logical_and(entry >= 0, entry < ROWS * B)
            slot = [
                jnp.where(inside, entry, slot[0]),
                jnp.where(inside, slot[0], slot[1]),
                jnp.where(inside, slot[1], slot[2]),
            ]
        place = lax.broadcasted_iota(i32, (B, B), 0)
        for j in range(SLOTS):
            hot[g, :, j * B : (j + 1) * B] = (place == (slot[j] & (B - 1))).astype(f32).astype(bf16)
        idx[g] = jnp.concatenate(slot + [jnp.full((8 - SLOTS, B), -1, i32)], axis=0)
        return carry

    lax.fori_loop(0, COLS, find, 0)

    def put_columns(values, v):
        hi, lo = halves(values)
        xs[v * 64 : v * 64 + 64, :] = jnp.concatenate([hi, lo], axis=0).astype(bf16)

    homes_arrived(cols, M, cm_send, cm_recv, lambda k: k % 4 == 0)
    for v in range(ROWS):
        turned = jnp.concatenate([cols[v, EMB : 2 * EMB, :], -cols[v, 0:EMB, :]], axis=0)
        hi, lo = halves(turned)
        right[v * B : (v + 1) * B, :] = jnp.concatenate([hi, hi, lo], axis=0).T.astype(bf16)

    def forward(g):
        picked = jnp.dot(xs[...], hot[g], preferred_element_type=f32)
        total = jnp.zeros((FEAT, B), f32)
        for j in range(SLOTS):
            window = idx[g, j : j + 1, :] >> 8
            part = jnp.zeros((2 * FEAT, B), f32)
            for v in range(ROWS):
                part = jnp.where(
                    window == v, picked[v * 64 : v * 64 + 64, j * B : (j + 1) * B], part
                )
            total = total + weight[g, j : j + 1, :] * (part[:FEAT] + part[FEAT:])
        return total

    def score_step(step, carry):
        t = own_core_first(step)
        g = order(t)

        @pl.when(jnp.logical_or(t % 2 == 1, jnp.logical_and(t >= 4, g != partner)))
        def _():
            row_arrival(rows, g, M, rm_send, rm_recv).wait_recv()

        @pl.when(jnp.logical_and(t % 2 == 0, t >= 4))
        def _():
            to_twin(t // 2, rows, M, rm_send, rm_recv).start()

        @pl.when(t == 4)
        def _():
            partner_block(S, rs_send, rs_recv, cs_send, cs_recv)
            row_arrival(rows, across(c), S, rs_send, rs_recv).wait_recv()
            for copy in s_relayed:
                copy.start()

        hi, lo = halves(rows[g, 0 : 2 * EMB, :])
        left[...] = jnp.concatenate([hi, lo, hi], axis=0).astype(bf16)
        eight = lax.broadcasted_iota(i32, (8, B), 0)
        gap = [idx[g, j : j + 1, :] - eight for j in range(SLOTS)]
        found = [jnp.zeros((8, B), f32) for _ in range(SLOTS)]
        for v in range(ROWS):
            score = jnp.dot(
                right[v * B : (v + 1) * B, :], left[...], preferred_element_type=f32
            )
            for t in range(B // 8):
                for j in range(SLOTS):
                    found[j] = jnp.where(
                        gap[j] == v * B + 8 * t, score[8 * t : 8 * t + 8], found[j]
                    )
        sums = jnp.zeros((1, B), f32)
        for j in range(SLOTS):
            value = jnp.tanh(3.0 * jnp.sum(found[j], axis=0, keepdims=True))
            value = jnp.where(idx[g, j : j + 1, :] >= 0, jnp.maximum(value, 0.0), 0.0)
            weight[g, j : j + 1, :] = value
            sums = sums + value
        f_part[g, FEAT:PART, :] = jnp.broadcast_to(sums, (8, B))
        return carry

    lax.fori_loop(0, COLS, score_step, 0)
    homes_arrived(cols, S, cs_send, cs_recv, lambda k: k % 4 == 0)
    for v in range(ROWS):
        put_columns(cols[v, 2 * EMB : ALL, :], v)

    def pair_sum(g, part, pair, send, recv):
        return pltpu.make_async_remote_copy(
            src_ref=part.at[g], dst_ref=pair.at[g], send_sem=send.at[g], recv_sem=recv.at[g],
            device_id=(r, twin(c)), device_id_type=MESH,
        )

    def forward_hop(part, pair, got, p_send, p_recv, send, recv, before):
        def for_twin(h, carry):
            before(h)
            blocks = [order(2 * (h * STEP + n) + 1) for n in range(STEP)]
            sums = [forward(g) for g in blocks]
            for g, total in zip(blocks, sums):
                part[g, 0:FEAT, :] = total
            for g in blocks:
                pair_sum(g, part, pair, p_send, p_recv).start()
            return carry

        def for_others(h, carry):
            before(h + ROWS // STEP)
            late = [(h * STEP + n + 1) % ROWS for n in range(STEP)]
            blocks = [order(2 * i) for i in late]
            sums = [forward(g) for g in blocks]
            for g, total in zip(blocks, sums):
                part[g, 0:FEAT, :] = total
            for g, i in zip(blocks, late):
                pair_sum(g, part, pair, p_send, p_recv).wait_recv()
                part[g] = part[g] + pair[g]

                @pl.when(i > 0)
                def _():
                    to_row(g, part.at[g], got, send, recv).start()

            return carry

        lax.fori_loop(0, ROWS // STEP, for_twin, 0)
        lax.fori_loop(0, ROWS // STEP, for_others, 0)

    def signals_on(h):
        for n in range(0, STEP, 2):
            t = h * STEP + n

            @pl.when(t >= 4)
            def _():
                @pl.when(order(t) != partner)
                def _():
                    row_arrival(rows, order(t), S, rs_send, rs_recv).wait_recv()

                to_twin(t // 2, rows, S, rs_send, rs_recv).start()

    forward_hop(f_part, f_pair, f_got, p_send, p_recv, f_send, f_recv, signals_on)

    def backward(rows_of, ready, with_degree):
        acc[...] = jnp.zeros_like(acc)
        depth = 528 if with_degree else 512

        def fill(g, n):
            x = rows_of(g)
            for j in range(SLOTS):
                window = idx[g, j : j + 1, :] >> 8
                value = weight[g, j : j + 1, :]
                hi, lo = halves(x * value)
                both = jnp.concatenate([hi, lo], axis=0)
                for v in range(ROWS):
                    st[n, v * 64 : v * 64 + 64, j * B : (j + 1) * B] = jnp.where(
                        window == v, both, 0.0
                    ).astype(bf16)
                if with_degree:
                    hi, lo = halves(value)
                    mine = lax.broadcasted_iota(i32, (8, B), 0) == window
                    st[n, 512:528, j * B : (j + 1) * B] = jnp.concatenate(
                        [jnp.where(mine, hi, 0.0), jnp.where(mine, lo, 0.0)], axis=0
                    ).astype(bf16)

        def step(h, carry):
            times = [own_core_first(h * STEP + n) for n in range(STEP)]
            blocks = [order(t) for t in times]
            for t, g in zip(times, blocks):
                ready(t, g)
            for n, g in enumerate(blocks):
                fill(g, n)
            total = acc[0:depth, :]
            for n, g in enumerate(blocks):
                total = total + lax.dot_general(
                    st[n, 0:depth, :], hot[g], (((1,), (1,)), ((), ())),
                    preferred_element_type=f32,
                )
            acc[0:depth, :] = total
            return carry

        lax.fori_loop(0, COLS // STEP, step, 0)

    def keep_backward(part, with_degree):
        for v in range(ROWS):
            part[v, 0:FEAT, :] = acc[v * 64 : v * 64 + 32, :] + acc[v * 64 + 32 : v * 64 + 64, :]
            if with_degree:
                part[v, FEAT:PART, :] = jnp.broadcast_to(
                    acc[512 + v : 513 + v, :] + acc[520 + v : 521 + v, :], (8, B)
                )

    def give_back(part, got, send, recv):
        def step(k, carry):
            @pl.when(jnp.logical_not(jnp.logical_and(same, k == q)))
            def _():
                to_homes(k, part.at[k], got, send, recv).start()

            return carry

        lax.fori_loop(0, ROWS, step, 0)

        @pl.when(same)
        def _():
            got[r] = part[q]

    def add_forward(part, got, send, recv):
        def step(n, total):
            k = (c + 2 * n) % COLS
            arrival(got, k, send, recv).wait_recv()
            return total + got[k]

        return lax.fori_loop(1, ROWS, step, part[c])

    def add_backward(got, send, recv):
        def step(k, total):
            @pl.when(jnp.logical_not(jnp.logical_and(same, k == r)))
            def _():
                arrival(got, k, send, recv).wait_recv()

            return total + got[k]

        return lax.fori_loop(0, ROWS, step, jnp.zeros(got.shape[1:], f32))

    def signal_ready(t, g):
        @pl.when(t % 2 == 1)
        def _():
            row_arrival(rows, g, S, rs_send, rs_recv).wait_recv()

    own_signal = lambda g: rows[g, 2 * EMB : ALL, :]
    backward(own_signal, signal_ready, True)
    keep_backward(b_part, True)
    give_back(b_part, b_got, b_send, b_recv)

    own = rows[c, 2 * EMB : ALL, :]
    summed = add_forward(f_part, f_got, f_send, f_recv)
    f_scale = GO / (1.0 + summed[FEAT : FEAT + 1])
    f_home[...] = KEEP * own + (summed[:FEAT] + own) * f_scale
    share_with_users(f_home, colx, c2_send, c2_recv)

    summed = add_backward(b_got, b_send, b_recv)
    b_scale = GO / (1.0 + summed[FEAT : FEAT + 1])
    rowx[c] = KEEP * own + (summed[:FEAT] + own) * b_scale
    A = pl.ds(0, FEAT)

    def to_chip(n):
        return pass_on((c + 2 * n) % COLS, rowx, c, rowx, A, n, r2_send, r2_recv)

    def on_to_twin(n):
        return pass_on(twin(c), rowx, (c + 2 * n) % COLS, rowx, A, ROWS + n, r2_send, r2_recv)

    for n in range(1, ROWS):
        to_chip(n).start()
    on_to_twin(0).start()

    homes_arrived(colx, pl.ds(0, FEAT), c2_send, c2_recv, lambda k: k == q)
    for v in range(ROWS):
        put_columns(colx[v], v)

    forward_hop(f_part2, f_pair2, f_got2, p2_send, p2_recv, f2_send, f2_recv, lambda h: None)

    for n in range(1, ROWS):
        row_arrival(rowx, (c + 2 * n) % COLS, A, r2_send, r2_recv).wait_recv()
        on_to_twin(n).start()

    def ready(t, g):
        @pl.when(t % 2 == 1)
        def _():
            row_arrival(rowx, g, A, r2_send, r2_recv).wait_recv()

    backward(lambda g: rowx[g], ready, False)
    keep_backward(b_part2, False)
    give_back(b_part2, b_got2, b2_send, b2_recv)

    fetches[6].wait()
    fetches[7].wait()
    first = f_home[...]
    summed = add_forward(f_part2, f_got2, f2_send, f2_recv)
    second = KEEP * own + (summed + first) * f_scale
    mixed = full_dot(wf[...], jnp.concatenate([own, first, second], axis=0))
    users_each(lambda k: to_users(k, f_home, colx, c2_send, c2_recv).wait_send())

    def sent(i, slot):
        home_to(i, slot, M, cm_send, cm_recv).wait_send()
        home_to(i, slot, S, cs_send, cs_recv).wait_send()

    homes_each(c, sent)
    homes_each(partner, sent)

    def sent_to_homes(k, carry):
        @pl.when(jnp.logical_not(jnp.logical_and(same, k == q)))
        def _():
            to_homes(k, b_part.at[k], b_got, b_send, b_recv).wait_send()
            to_homes(k, b_part2.at[k], b_got2, b2_send, b2_recv).wait_send()

        return carry

    def sent_to_row(n, carry):
        k = (c + 2 * n) % COLS
        to_row(k, f_part.at[k], f_got, f_send, f_recv).wait_send()
        to_row(k, f_part2.at[k], f_got2, f2_send, f2_recv).wait_send()
        to_chip(n).wait_send()
        return carry

    def sent_to_pair(n, carry):
        k = (twin(c) + 2 * n) % COLS
        pair_sum(k, f_part, f_pair, p_send, p_recv).wait_send()
        pair_sum(k, f_part2, f_pair2, p2_send, p2_recv).wait_send()
        on_to_twin(n).wait_send()
        return carry

    lax.fori_loop(0, ROWS, sent_to_pair, 0)
    lax.fori_loop(0, ROWS, sent_to_homes, 0)
    lax.fori_loop(1, ROWS, sent_to_row, 0)
    for copy in m_mine + m_relayed + s_mine + s_relayed:
        copy.wait_send()

    def sent_to_twin(i, carry):
        to_twin(i, rows, M, rm_send, rm_recv).wait_send()
        to_twin(i, rows, S, rs_send, rs_recv).wait_send()
        return carry

    lax.fori_loop(2, ROWS, sent_to_twin, 0)

    first = rowx[c]
    mixed = mixed + full_dot(wb[:, 0 : 2 * FEAT], jnp.concatenate([own, first], axis=0))
    summed = add_backward(b_got2, b2_send, b2_recv)
    second = KEEP * own + (summed + first) * b_scale
    out[...] = mixed + full_dot(wb[:, 2 * FEAT : 3 * FEAT], second)


def per_device(*args):
    vmem = pltpu.VMEM
    keep_count = args[5].shape[0]
    dma = pltpu.SemaphoreType.DMA
    scratch = [
        vmem((EMB, B), f32), vmem((EMB, B), f32), vmem((EMB, EMB), f32), vmem((EMB, EMB), f32),
        vmem((keep_count, COLS * B), i32), vmem((FEAT, 3 * FEAT), f32), vmem((FEAT, 3 * FEAT), f32),
        vmem((COLS, ALL, B), f32),
        vmem((ROWS, ALL, B), f32),
        vmem((ROWS * B, 6 * EMB), bf16),
        vmem((6 * EMB, B), bf16),
        vmem((512, B), bf16),
        vmem((STEP, 528, SLOTS * B), bf16),
        vmem((COLS, B, SLOTS * B), bf16),
        vmem((COLS, 8, B), i32),
        vmem((COLS, 8, B), f32),
        vmem((528, B), f32),
        vmem((COLS, PART, B), f32), vmem((COLS, PART, B), f32),
        vmem((COLS, PART, B), f32),
        vmem((ROWS, PART, B), f32), vmem((ROWS, PART, B), f32),
        vmem((FEAT, B), f32),
        vmem((ROWS, FEAT, B), f32), vmem((COLS, FEAT, B), f32),
        vmem((COLS, FEAT, B), f32), vmem((COLS, FEAT, B), f32),
        vmem((COLS, FEAT, B), f32),
        vmem((ROWS, FEAT, B), f32), vmem((ROWS, FEAT, B), f32),
        dma((8,)),
    ]
    for count in (ROWS, ROWS, COLS, COLS, COLS, ROWS, ROWS, COLS, COLS, ROWS, COLS, COLS):
        scratch += [dma((count,)), dma((count,))]
    return pl.pallas_call(
        kernel,
        out_shape=jax.ShapeDtypeStruct((FEAT, B), f32),
        in_specs=[pl.BlockSpec(memory_space=pl.ANY)] * 8,
        out_specs=pl.BlockSpec(memory_space=pltpu.VMEM),
        scratch_shapes=scratch,
        compiler_params=pltpu.CompilerParams(
            collective_id=0, has_side_effects=True, vmem_limit_bytes=VMEM_BYTES
        ),
        name="graph_layer",
    )(*args[:6], args[6].T, args[7].T)


def solution(mesh):
    placed = (
        P(None, ("row", "col")),
        P(None, ("row", "col")),
        P(None, ("row", "col")),
        P(),
        P(),
        P(None, "row"),
        P(),
        P(),
    )
    return jax.shard_map(
        per_device, mesh=mesh, in_specs=placed, out_specs=P(None, ("row", "col")), check_vma=False
    )
```
